32 devices in a mesh: dp: 8 (over z, y), mp: 4 (over x, core).
Axes of the slice: x: 2, y: 2, z: 4, core: 2. Of those that a mesh axis runs over, the one named last changes fastest.
Arguments:
- activations: bfloat16 [4096, 2048], P('dp'), may hold values from -6 to 6
- cotangent: bfloat16 [4096, 2048], P('dp'), may hold values from -6 to 6
- positions: int32 [4096], P('dp'), may hold values from -1 to 255, as said below
- w_qkv: float32 [2, 3, 2048, 2048], P(None, None, 'dp', 'mp'), may hold values from -0.125 to 0.125
- w_out: float32 [2, 2048, 2048], P(None, 'mp', 'dp'), may hold values from -0.5 to 0.5
- w_up: float32 [2, 2048, 8192], P(None, 'dp', 'mp'), may hold values from -0.125 to 0.125
- w_down: float32 [2, 8192, 2048], P(None, 'mp', 'dp'), may hold values from -0.0625 to 0.0625
- vec_model: float32 [2, 4, 2048], P(None, None, 'dp')
- vec_head: float32 [2, 3, 2048], P(None, None, ('mp', 'dp')), may hold values from -2 to 2
- vec_ffn: float32 [2, 8192], P(None, ('mp', 'dp')), may hold values from -2 to 2
- first_qkv: float32 [2, 3, 2048, 2048], P(None, None, 'dp', 'mp'), may hold values from -32 to 32
- first_out: float32 [2, 2048, 2048], P(None, 'mp', 'dp'), may hold values from -14 to 14
- first_up: float32 [2, 2048, 8192], P(None, 'dp', 'mp'), may hold values from -14 to 14
- first_down: float32 [2, 8192, 2048], P(None, 'mp', 'dp'), may hold values from -20 to 20
- first_model: float32 [2, 4, 2048], P(None, None, 'dp'), may hold values from -40 to 40
- first_head: float32 [2, 3, 2048], P(None, None, ('mp', 'dp')), may hold values from -32 to 32
- first_ffn: float32 [2, 8192], P(None, ('mp', 'dp')), may hold values from -14 to 14
- second_qkv: float32 [2, 3, 2048, 2048], P(None, None, 'dp', 'mp'), may hold values from 108.544 to 430.08
- second_out: float32 [2, 2048, 2048], P(None, 'mp', 'dp'), may hold values from 21.7088 to 86.016
- second_up: float32 [2, 2048, 8192], P(None, 'dp', 'mp'), may hold values from 21.7088 to 86.016
- second_down: float32 [2, 8192, 2048], P(None, 'mp', 'dp'), may hold values from 54.272 to 215.04
- second_model: float32 [2, 4, 2048], P(None, None, 'dp'), may hold values from 217.088 to 860.16
- second_head: float32 [2, 3, 2048], P(None, None, ('mp', 'dp')), may hold values from 108.544 to 430.08
- second_ffn: float32 [2, 8192], P(None, ('mp', 'dp')), may hold values from 21.7088 to 86.016
Outputs:
- result: float32 [4096, 2048], P('dp')
- grad_input: float32 [4096, 2048], P('dp')
- grad_qkv: float32 [2, 3, 2048, 2048], P(None, None, 'dp', 'mp')
- next_first_qkv: float32 [2, 3, 2048, 2048], P(None, None, 'dp', 'mp')
- next_second_qkv: float32 [2, 3, 2048, 2048], P(None, None, 'dp', 'mp')
- next_w_qkv: float32 [2, 3, 2048, 2048], P(None, None, 'dp', 'mp')
- grad_out: float32 [2, 2048, 2048], P(None, 'mp', 'dp')
- next_first_out: float32 [2, 2048, 2048], P(None, 'mp', 'dp')
- next_second_out: float32 [2, 2048, 2048], P(None, 'mp', 'dp')
- next_w_out: float32 [2, 2048, 2048], P(None, 'mp', 'dp')
- grad_up: float32 [2, 2048, 8192], P(None, 'dp', 'mp')
- next_first_up: float32 [2, 2048, 8192], P(None, 'dp', 'mp')
- next_second_up: float32 [2, 2048, 8192], P(None, 'dp', 'mp')
- next_w_up: float32 [2, 2048, 8192], P(None, 'dp', 'mp')
- grad_down: float32 [2, 8192, 2048], P(None, 'mp', 'dp')
- next_first_down: float32 [2, 8192, 2048], P(None, 'mp', 'dp')
- next_second_down: float32 [2, 8192, 2048], P(None, 'mp', 'dp')
- next_w_down: float32 [2, 8192, 2048], P(None, 'mp', 'dp')
- grad_model: float32 [2, 4, 2048], P(None, None, 'dp')
- next_first_model: float32 [2, 4, 2048], P(None, None, 'dp')
- next_second_model: float32 [2, 4, 2048], P(None, None, 'dp')
- next_vec_model: float32 [2, 4, 2048], P(None, None, 'dp')
- grad_head: float32 [2, 3, 2048], P(None, None, ('mp', 'dp'))
- next_first_head: float32 [2, 3, 2048], P(None, None, ('mp', 'dp'))
- next_second_head: float32 [2, 3, 2048], P(None, None, ('mp', 'dp'))
- next_vec_head: float32 [2, 3, 2048], P(None, None, ('mp', 'dp'))
- grad_ffn: float32 [2, 8192], P(None, ('mp', 'dp'))
- next_first_ffn: float32 [2, 8192], P(None, ('mp', 'dp'))
- next_second_ffn: float32 [2, 8192], P(None, ('mp', 'dp'))
- next_vec_ffn: float32 [2, 8192], P(None, ('mp', 'dp'))
The draws below stay inside these ranges and needn't reach their ends.
Inputs may be any that keep to these rules, and one draw needn't show every extreme that they name: Each aligned block of 256 slots holds whole sequences one after another from its start, positions counting 0, 1, 2, ... in each, then empty slots; at least half of every block's slots are used, and some block holds one sequence of 256 tokens.
All inputs are finite; a program needn't handle non-finite values.
Results may differ from the reference program's by a relative error of at most 0.025.
Values may be sent and summed in bfloat16 or wider, within the bound.
No kernel may reach another device: no remote copies, remote signals or barrier semaphores. Data moves between devices by JAX's collectives and lax.ppermute only.
A program may use at most 384 MiB of HBM per device.

```python
import math
import jax
import jax.numpy as jnp
from jax import lax

D = 2048
HEADS = 32
HEAD_DIM = 64
ROT = 32
FF = 8192
LAYERS = 2
STEP = 10
ROWS = 256
TOKENS = 4096


def draw_positions(key, part):
    key = jax.random.fold_in(key, 11)
    buffers = TOKENS // ROWS
    buffer_index = jnp.arange(buffers, dtype=jnp.int32)
    lengths = jax.random.randint(jax.random.fold_in(key, 1), (buffers,), ROWS // 2, ROWS + 1)
    lengths = jnp.where(buffer_index == 0, ROWS, jnp.where(buffer_index == 1, ROWS // 2, lengths))
    columns = jnp.arange(ROWS, dtype=jnp.int32)[None, :]
    start_flags = jax.random.randint(jax.random.fold_in(key, 2), (buffers, ROWS), 0, ROWS) < 3
    start_flags = start_flags & (buffer_index[:, None] != 0) | (columns == 0)
    start_marks = jnp.where(start_flags, columns, 0)
    starts = lax.cummax(start_marks, axis=1)
    places = jnp.where(columns < lengths[:, None], columns - starts, -1)
    return places.reshape(-1).astype(jnp.int32)


def draw_vec_model(key, part):
    key = jax.random.fold_in(key, 5)
    spread = jax.random.normal(key, (LAYERS, 4, D)) * 0.3
    level = jnp.arange(4, dtype=jnp.int32)[None, :, None] == 0
    return jnp.where(level, 1.0 + spread, spread).astype(jnp.float32)


def block_levels(key, dims, cuts, least, largest):
    def one(axis_at, blocks):
        draws = jax.random.uniform(jax.random.fold_in(jax.random.fold_in(key, 6), axis_at), (blocks,), jnp.float32, least / len(cuts), largest / len(cuts))
        return jnp.repeat(jnp.exp(draws), dims[axis_at] // blocks).reshape((-1,) + (1,) * (len(dims) - axis_at - 1))

    factor_of = one(*cuts[0])
    for cut in cuts[1:]:
        factor_of = factor_of * one(*cut)
    return factor_of


def scatter_about(stream_key, shape, scale, reach, split=(), kind=jnp.bfloat16):
    drawn = scale * jax.random.normal(stream_key, shape, jnp.float32)
    if split:
        drawn = drawn * block_levels(stream_key, shape, split, -0.22, 0.18)
    return jnp.clip(drawn, -reach, reach).astype(kind)


def setup_inputs(seed: int = 0) -> dict:
    key_list = jax.random.split(jax.random.key(seed), 25)
    return {
        "activations": scatter_about(key_list[0], (TOKENS, D), 1.0, 6.0, ((0, 8),)),
        "cotangent": scatter_about(key_list[1], (TOKENS, D), 1.0, 6.0, ((0, 8),)),
        "positions": draw_positions(jax.random.fold_in(key_list[24], 71), 0),
        "w_qkv": scatter_about(key_list[3], (LAYERS, 3, D, D), D ** -0.5, 0.125, ((2, 8), (3, 4)), jnp.float32),
        "w_out": scatter_about(key_list[4], (LAYERS, D, D), (D // 16) ** -0.5, 0.5, ((1, 4), (2, 8)), jnp.float32),
        "w_up": scatter_about(key_list[5], (LAYERS, D, FF), D ** -0.5, 0.125, ((1, 8), (2, 4)), jnp.float32),
        "w_down": scatter_about(key_list[6], (LAYERS, FF, D), FF ** -0.5, 0.0625, ((1, 4), (2, 8)), jnp.float32),
        "vec_model": draw_vec_model(jax.random.fold_in(key_list[24], 71), 0),
        "vec_head": scatter_about(key_list[8], (LAYERS, 3, D), 0.3, 2.0, ((2, 32),), jnp.float32),
        "vec_ffn": scatter_about(key_list[9], (LAYERS, FF), 0.3, 2.0, ((1, 32),), jnp.float32),
        "first_qkv": scatter_about(key_list[10], (LAYERS, 3, D, D), (0.11 * (0.5 * TOKENS) ** 0.5), 32.0, ((2, 8), (3, 4)), jnp.float32),
        "first_out": scatter_about(key_list[11], (LAYERS, D, D), (0.11 * (0.1 * TOKENS) ** 0.5), 14.0, ((1, 4), (2, 8)), jnp.float32),
        "first_up": scatter_about(key_list[12], (LAYERS, D, FF), (0.11 * (0.1 * TOKENS) ** 0.5), 14.0, ((1, 8), (2, 4)), jnp.float32),
        "first_down": scatter_about(key_list[13], (LAYERS, FF, D), (0.11 * (0.25 * TOKENS) ** 0.5), 20.0, ((1, 4), (2, 8)), jnp.float32),
        "first_model": scatter_about(key_list[14], (LAYERS, 4, D), (0.11 * TOKENS ** 0.5), 40.0, ((2, 8),), jnp.float32),
        "first_head": scatter_about(key_list[15], (LAYERS, 3, D), (0.11 * (0.5 * TOKENS) ** 0.5), 32.0, ((2, 32),), jnp.float32),
        "first_ffn": scatter_about(key_list[16], (LAYERS, FF), (0.11 * (0.1 * TOKENS) ** 0.5), 14.0, ((1, 32),), jnp.float32),
        "second_qkv": jnp.clip(jnp.exp(math.log(430.08) - 1.3768156 * jax.random.uniform(key_list[17], (LAYERS, 3, D, D), jnp.float32) ** block_levels(key_list[17], (LAYERS, 3, D, D), ((2, 8), (3, 4)), -0.2, 0.2)), 108.544, 430.08),
        "second_out": jnp.clip(jnp.exp(math.log(86.016) - 1.37681563 * jax.random.uniform(key_list[18], (LAYERS, D, D), jnp.float32) ** block_levels(key_list[18], (LAYERS, D, D), ((1, 4), (2, 8)), -0.2, 0.2)), 21.7088, 86.016),
        "second_up": jnp.clip(jnp.exp(math.log(86.016) - 1.37681563 * jax.random.uniform(key_list[19], (LAYERS, D, FF), jnp.float32) ** block_levels(key_list[19], (LAYERS, D, FF), ((1, 8), (2, 4)), -0.2, 0.2)), 21.7088, 86.016),
        "second_down": jnp.clip(jnp.exp(math.log(215.04) - 1.3768156 * jax.random.uniform(key_list[20], (LAYERS, FF, D), jnp.float32) ** block_levels(key_list[20], (LAYERS, FF, D), ((1, 4), (2, 8)), -0.2, 0.2)), 54.272, 215.04),
        "second_model": jnp.clip(jnp.exp(math.log(860.16) - 1.3768156 * jax.random.uniform(key_list[21], (LAYERS, 4, D), jnp.float32) ** block_levels(key_list[21], (LAYERS, 4, D), ((2, 8),), -0.2, 0.2)), 217.088, 860.16),
        "second_head": jnp.clip(jnp.exp(math.log(430.08) - 1.3768156 * jax.random.uniform(key_list[22], (LAYERS, 3, D), jnp.float32) ** block_levels(key_list[22], (LAYERS, 3, D), ((2, 32),), -0.2, 0.2)), 108.544, 430.08),
        "second_ffn": jnp.clip(jnp.exp(math.log(86.016) - 1.37681563 * jax.random.uniform(key_list[23], (LAYERS, FF), jnp.float32) ** block_levels(key_list[23], (LAYERS, FF), ((1, 32),), -0.2, 0.2)), 21.7088, 86.016),
    }


BETA_ONE = 0.9
BETA_TWO = 0.95
ADAM_EPS = 1e-08
DECAY = 0.1
NORM_EPS = 1e-05
MASKED = -1e+30
HIGHEST = lax.Precision.HIGHEST

@jax.custom_vjp
def low(v):
    return lax.optimization_barrier(v.astype(jnp.bfloat16)).astype(jnp.float32)

@jax.custom_vjp
def low_back(v):
    return v

def low_keep(v):
    return (low(v), None)

def low_pass(kept, grad):
    return (grad,)

def back_keep(v):
    return (v, None)

def back_low(kept, grad):
    return (low(grad),)
low.defvjp(low_keep, low_pass)
low_back.defvjp(back_keep, back_low)

def layer_norm(hidden, gain, shift):
    centre = hidden - lax.optimization_barrier(jnp.mean(hidden, -1, keepdims=True))
    spread = lax.optimization_barrier(jnp.mean(centre * centre, -1, keepdims=True))
    return centre * lax.rsqrt(spread + NORM_EPS) * gain + shift

def tables(positions):
    places = jnp.maximum(positions, 0).astype(jnp.float32)
    frequency = 10000.0 ** (-(2.0 / ROT) * jnp.arange(ROT // 2).astype(jnp.float32))
    angles = places[:, None] * frequency[None, :]
    return (jnp.cos(angles), jnp.sin(angles))

def rotate(values, cosine, sine):
    half_rot = cosine.shape[-1]
    lower_half = values[..., :half_rot]
    upper_half = values[..., half_rot:2 * half_rot]
    remain = values[..., 2 * half_rot:]
    cos_cast = cosine[:, None, :]
    sin_cast = sine[:, None, :]
    return jnp.concatenate([lower_half * cos_cast - upper_half * sin_cast, upper_half * cos_cast + lower_half * sin_cast, remain], -1)

def visible(places):
    count = places.shape[-1]
    row_ids = jnp.arange(count, dtype=jnp.int32)[:, None]
    col_ids = jnp.arange(count, dtype=jnp.int32)[None, :]
    starts = row_ids - jnp.maximum(places, 0)[..., :, None]
    return (col_ids <= row_ids) & (col_ids >= starts)

def attend(pieces):
    queries, keys_rot, values, places = pieces
    score_scale = HEAD_DIM ** (-0.5)
    scores = low_back(jnp.einsum('qhe,khe->hqk', queries, keys_rot, precision=HIGHEST) * score_scale)
    scores = jnp.where(visible(places)[None], scores, MASKED)
    row_max = lax.optimization_barrier(jnp.max(scores, -1, keepdims=True))
    exponent = jnp.exp(scores - row_max)
    attn_probs = exponent / lax.optimization_barrier(jnp.sum(exponent, -1, keepdims=True))
    return jnp.einsum('hqk,khe->qhe', low(attn_probs), values, precision=HIGHEST)

def one_layer(hidden, weights, cosine, sine, positions):
    weights_qkv, weights_out, weights_up, weights_down, model_vec, head_vec, ffn_vec = [low(piece) for piece in weights]
    tokens_all = hidden.shape[0]
    normed = low(layer_norm(hidden, model_vec[0], model_vec[1]))
    project = jnp.einsum('rd,cde->cre', normed, weights_qkv, precision=HIGHEST) + head_vec[:, None, :]
    project = low_back(project).reshape(3, tokens_all, HEADS, HEAD_DIM)
    queries = low(rotate(project[0], cosine, sine))
    keys_rot = low(rotate(project[1], cosine, sine))
    values = low(project[2])
    blocks = tokens_all // ROWS
    shape_four = (blocks, ROWS, HEADS, HEAD_DIM)
    mixture = lax.map(jax.checkpoint(attend), (queries.reshape(shape_four), keys_rot.reshape(shape_four), values.reshape(shape_four), positions.reshape(blocks, ROWS)))
    heads_out = low(low_back(mixture.reshape(tokens_all, D)))
    attention = jnp.dot(heads_out, weights_out, precision=HIGHEST)
    gate_in = low_back(jnp.dot(normed, weights_up, precision=HIGHEST) + ffn_vec)
    activated = low(jax.nn.gelu(gate_in, approximate=True))
    branch = low_back(attention + jnp.dot(activated, weights_down, precision=HIGHEST))
    return hidden + branch + model_vec[2] + model_vec[3]

def adamw(weight, grad, first, second, rate, decay):
    first_new = BETA_ONE * first + (1.0 - BETA_ONE) * grad
    second_new = BETA_TWO * second + (1.0 - BETA_TWO) * grad * grad
    first_hat = first_new / (1.0 - BETA_ONE ** STEP)
    second_hat = second_new / (1.0 - BETA_TWO ** STEP)
    weight_new = weight - rate * (first_hat / (jnp.sqrt(second_hat) + ADAM_EPS) + decay * weight)
    return (first_new, second_new, weight_new)

def reference(activations, cotangent, positions, w_qkv, w_out, w_up, w_down, vec_model, vec_head, vec_ffn, first_qkv, first_out, first_up, first_down, first_model, first_head, first_ffn, second_qkv, second_out, second_up, second_down, second_model, second_head, second_ffn):
    cosine, sine = tables(positions)
    params = (w_qkv, w_out, w_up, w_down, vec_model, vec_head, vec_ffn)

    def forward(start, weights):
        hidden = start
        for layer_index in range(LAYERS):
            hidden = one_layer(hidden, [piece[layer_index] for piece in weights], cosine, sine, positions)
        return hidden
    start = activations.astype(jnp.float32)
    result, pullback = jax.vjp(forward, start, params)
    live = (positions >= 0).astype(jnp.float32)[:, None]
    grad_input, grads = pullback(cotangent.astype(jnp.float32) * live)
    grad_qkv, grad_out, grad_up, grad_down, grad_model, grad_head, grad_ffn = grads
    rate_in = 3.0 / math.sqrt(D)
    next_first_qkv, next_second_qkv, next_w_qkv = adamw(w_qkv, grad_qkv, first_qkv, second_qkv, rate_in, DECAY)
    next_first_out, next_second_out, next_w_out = adamw(w_out, grad_out, first_out, second_out, 12.0 / math.sqrt(D), DECAY)
    next_first_up, next_second_up, next_w_up = adamw(w_up, grad_up, first_up, second_up, rate_in, DECAY)
    next_first_down, next_second_down, next_w_down = adamw(w_down, grad_down, first_down, second_down, 3.0 / math.sqrt(FF), DECAY)
    next_first_model, next_second_model, next_vec_model = adamw(vec_model, grad_model, first_model, second_model, 0.6, 0.0)
    next_first_head, next_second_head, next_vec_head = adamw(vec_head, grad_head, first_head, second_head, 0.6, 0.0)
    next_first_ffn, next_second_ffn, next_vec_ffn = adamw(vec_ffn, grad_ffn, first_ffn, second_ffn, 0.6, 0.0)
    return (result, grad_input, grad_qkv, next_first_qkv, next_second_qkv, next_w_qkv, grad_out, next_first_out, next_second_out, next_w_out, grad_up, next_first_up, next_second_up, next_w_up, grad_down, next_first_down, next_second_down, next_w_down, grad_model, next_first_model, next_second_model, next_vec_model, grad_head, next_first_head, next_second_head, next_vec_head, grad_ffn, next_first_ffn, next_second_ffn, next_vec_ffn)
```

```python
import math

import jax
import jax.numpy as jnp
import numpy as np
from jax import lax
from jax.experimental import pallas as pl
from jax.experimental.pallas import tpu as pltpu
from jax.sharding import Mesh
from jax.sharding import PartitionSpec as P

D = 2048
HEAD_DIM = 64
ROT = 32
FF = 8192
LAYERS = 2
STEP = 10
ROWS = 256
ZS = 4
HALF = 128
PAIR = 2 * HEAD_DIM

BETA_ONE = 0.9
BETA_TWO = 0.95
ADAM_EPS = 1e-08
DECAY = 0.1
NORM_EPS = 1e-05
MASKED = -1e30
BF = jnp.bfloat16
F32 = jnp.float32
VMEM_LIMIT = 58 * 2**20
SMALL_COST = pl.CostEstimate(flops=1024, bytes_accessed=1024, transcendentals=0)


def shift_z(array, step):
    return lax.ppermute(array, "z", [(i, (i + step) % ZS) for i in range(ZS)])


def swap(array, axis):
    return lax.ppermute(array, axis, [(0, 1), (1, 0)])


def dot_nt(left, right):
    return lax.dot_general(left, right, (((1,), (1,)), ((), ())), preferred_element_type=F32)


def dot_nn(left, right):
    return lax.dot_general(left, right, (((1,), (0,)), ((), ())), preferred_element_type=F32)


def dot_tn(left, right):
    return lax.dot_general(left, right, (((0,), (0,)), ((), ())), preferred_element_type=F32)


def turn(values, table):
    return (
        values * table[:, :PAIR]
        + pltpu.roll(values, PAIR - ROT // 2, 1) * table[:, PAIR : 2 * PAIR]
        + pltpu.roll(values, ROT // 2, 1) * table[:, 2 * PAIR :]
    )


def turn_back(grads, table):
    return (
        grads * table[:, :PAIR]
        - pltpu.roll(grads, PAIR - ROT // 2, 1) * table[:, PAIR : 2 * PAIR]
        - pltpu.roll(grads, ROT // 2, 1) * table[:, 2 * PAIR :]
    )


def low_lanes():
    return lax.broadcasted_iota(jnp.int32, (ROWS, PAIR), 1) < HEAD_DIM


def head_only(values, head):
    low_half = low_lanes()
    mine = low_half if head == 0 else jnp.logical_not(low_half)
    return jnp.where(mine, values, jnp.zeros_like(values))


def attend(queries, keys, values, mask):
    outs, logs = [], []
    for head in range(2):
        scores = dot_nt(head_only(queries, head), keys) + mask
        top = jnp.max(scores, -1, keepdims=True)
        exponent = jnp.exp(scores - top)
        total = jnp.sum(exponent, -1, keepdims=True)
        outs.append(dot_nn((exponent * (1.0 / total)).astype(BF), values))
        logs.append(jnp.broadcast_to(top + jnp.log(total), (ROWS, PAIR)))
    low_half = low_lanes()
    return jnp.where(low_half, *outs), jnp.where(low_half, *logs)


def attend_back(queries, keys, values, logs, grad, mask):
    grads = []
    for head in range(2):
        at = head * HEAD_DIM
        scores = dot_nt(head_only(queries, head), keys) + mask
        probs = jnp.exp(scores - logs[:, at : at + 1])
        grad_probs = dot_nt(head_only(grad, head), values)
        row_dot = jnp.sum(probs * grad_probs, -1, keepdims=True)
        grad_scores = (probs * (grad_probs - row_dot)).astype(BF)
        grads.append(
            (
                dot_nn(grad_scores, keys),
                dot_tn(grad_scores, queries),
                dot_tn(probs.astype(BF), grad),
            )
        )
    low_half = low_lanes()
    return [jnp.where(low_half, one, two) for one, two in zip(*grads)]


def cut_of(kind):
    return {"front": 3 * PAIR, "back": 2 * PAIR, "both": 6 * PAIR}[kind]


def nt_cols(left, segment):
    chunks, first, last = segment
    total, at = 0.0, 0
    for chunk in chunks:
        total = total + dot_nt(left[:, at : at + chunk.shape[1]], chunk[first:last])
        at += chunk.shape[1]
    return total


def nn_cols(left, segment):
    chunks, first, last = segment
    parts = [dot_nn(left, chunk[first:last]) for chunk in chunks]
    return parts[0] if len(parts) == 1 else jnp.concatenate(parts, 1)


def times_t(left, weights, x):
    near, on_y, on_x, far = weights
    half = left.shape[1] // 2
    lower, upper = left[:, :half], left[:, half:]
    if x == 0:
        return nt_cols(lower, near) + nt_cols(upper, on_y)
    parts = [nt_cols(upper, segment) for segment in far]
    return nt_cols(lower, on_x) + (parts[0] if len(parts) == 1 else jnp.concatenate(parts, 1))


def times(left, weights):
    near, on_y, on_x, far = weights
    n = near[2] - near[1]
    own, other = left[:, :n], left[:, n:]
    lower = nn_cols(own, near) + nn_cols(other, on_x)
    upper, at = nn_cols(own, on_y), 0
    for segment in far:
        rows = segment[2] - segment[1]
        upper = upper + nn_cols(other[:, at : at + rows], segment)
        at += rows
    return lower, upper


def bind(layout, refs):
    chunks = lambda part: (tuple(refs[at] for at in part[0]), part[1], part[2])
    near, on_y, on_x, far = layout
    return chunks(near), chunks(on_y), chunks(on_x), [chunks(part) for part in far]


def lanes_of(z_ref, k, y, dd):
    return pl.ds(pl.multiple_of(y * ZS * dd + (z_ref[0] - k + ZS) % ZS * dd, dd), dd)


def take_rows(z_ref, sources, relative, target=None):
    dd = relative.shape[1] // (2 * ZS)
    for slot in range(ZS):

        @pl.when(pl.program_id(0) == slot)
        def _():
            for core in range(2):
                source = sources[core * ZS + slot]
                rows = slice(core * HALF, (core + 1) * HALF)
                for y in range(2):
                    for k in range(ZS):
                        to = (y * ZS + k) * dd
                        relative[rows, to : to + dd] = source[:, lanes_of(z_ref, k, y, dd)]
                if target is not None:
                    target[core, 0] = source[...]


def put(ref, at, value):
    width = value.shape[1]
    ref[:, :, :, at : at + width] = value.astype(ref.dtype).reshape(2, 1, HALF, width)


def get(ref, at, width):
    return ref[:, :, :, at : at + width].reshape(ROWS, width)


def put_parts(z_ref, halves, own_ref, other_ref):
    for y, value in enumerate(halves):
        dd = value.shape[1] // ZS
        for k in range(ZS):
            lanes = lanes_of(z_ref, k, y, dd)
            part = value[:, k * dd : (k + 1) * dd].astype(BF)
            own_ref[0, :, lanes] = part[:HALF]
            other_ref[0, :, lanes] = part[HALF:]


def front_kernel(layouts, count, z_ref, *refs):
    rows, refs = refs[:8], refs[8:]
    weights, refs = refs[:count], refs[count:]
    fronts = bind(layouts[0], weights)
    bias_ref, table_ref, mask_ref, normed_ref, qkv_ref, log_ref, left_ref, slope_ref = refs[:8]
    relative = refs[-1]
    take_rows(z_ref, rows, relative, normed_ref)
    normed = relative[...]
    table = get(table_ref, 0, 3 * PAIR)
    n = fronts[0][2] - fronts[0][1]
    ffn_n = n - 3 * PAIR
    root = math.sqrt(2.0 / math.pi)
    for x in range(2):
        both = times_t(normed, fronts, x) + bias_ref[:, x * n : (x + 1) * n]
        gate = both[:, 3 * PAIR :]
        square = gate * gate
        bend = jnp.tanh(root * gate * (1.0 + 0.044715 * square))
        half_up = 0.5 + 0.5 * bend
        put(left_ref, x * (PAIR + ffn_n) + PAIR, gate * half_up)
        slope = half_up + (0.5 * gate) * (1.0 - bend * bend) * (
            root + (3.0 * 0.044715 * root) * square
        )
        put(slope_ref, x * ffn_n, slope)
        queries = turn(both[:, :PAIR], table).astype(BF) * jnp.asarray(HEAD_DIM**-0.5, BF)
        keys = turn(both[:, PAIR : 2 * PAIR], table).astype(BF)
        values = both[:, 2 * PAIR : 3 * PAIR].astype(BF)
        out, logs = attend(queries, keys, values, mask_ref[0])
        for which, value in enumerate((queries, keys, values)):
            put(qkv_ref, (3 * x + which) * PAIR, value)
        put(left_ref, x * (PAIR + ffn_n), out)
        put(log_ref, x * PAIR, logs)
    if len(layouts) > 1:
        backs = bind(layouts[1], weights)
        put_parts(z_ref, times(get(left_ref, 0, left_ref.shape[-1]), backs), *refs[8:10])


def slot_spec(width):
    return pl.BlockSpec((2, 1, HALF, width), lambda k: (0, k, 0, 0))


def fixed(shape):
    return pl.BlockSpec(
        shape, lambda *_: (0,) * len(shape), pipeline_mode=pl.Buffered(buffer_count=1)
    )


def slot_shape(width, kind):
    return jax.ShapeDtypeStruct((2, ZS, HALF, width), kind)


SMEM_SPEC = pl.BlockSpec(memory_space=pltpu.SMEM)
ANY_SPEC = pl.BlockSpec(memory_space=pl.ANY)
MASK_SPEC = pl.BlockSpec((1, ROWS, ROWS), lambda k: (k, 0, 0))
PART_SPEC = pl.BlockSpec((1, HALF, D), lambda k: (k, 0, 0))
PART_SHAPE = jax.ShapeDtypeStruct((ZS, HALF, D), BF)
ALL_ROWS = 2 * ZS * HALF
RELATIVE = pltpu.VMEM((ROWS, D), BF)


def front(z_array, rows, layouts, weights, bias, table, mask):
    n = bias.shape[1] // 2
    ffn_n = n - 3 * PAIR
    widths = [(D, BF), (6 * PAIR, BF), (2 * PAIR, F32), (2 * (PAIR + ffn_n), BF), (2 * ffn_n, BF)]
    parts = 2 * (len(layouts) - 1)
    return pl.pallas_call(
        lambda *refs: front_kernel(layouts, len(weights), *refs),
        grid=(ZS,),
        in_specs=[SMEM_SPEC]
        + [fixed(a.shape) for a in (*rows, *weights, bias)]
        + [slot_spec(3 * PAIR), MASK_SPEC],
        out_specs=[slot_spec(width) for width, _ in widths] + [PART_SPEC] * parts,
        out_shape=[slot_shape(*pair) for pair in widths] + [PART_SHAPE] * parts,
        scratch_shapes=[RELATIVE],
        compiler_params=pltpu.CompilerParams(vmem_limit_bytes=VMEM_LIMIT),
        cost_estimate=SMALL_COST,
        name="block_front",
    )(z_array, *rows, *weights, bias, table, mask)


def back_kernel(layout, z_ref, left_ref, *refs):
    left = get(left_ref, 0, left_ref.shape[-1])
    put_parts(z_ref, times(left, bind(layout, refs[:-2])), *refs[-2:])


def back(z_array, left, layout, weights):
    return pl.pallas_call(
        lambda *refs: back_kernel(layout, *refs),
        grid=(ZS,),
        in_specs=[SMEM_SPEC, slot_spec(left.shape[-1])] + [fixed(a.shape) for a in weights],
        out_specs=[PART_SPEC] * 2,
        out_shape=[PART_SHAPE] * 2,
        compiler_params=pltpu.CompilerParams(vmem_limit_bytes=VMEM_LIMIT),
        cost_estimate=SMALL_COST,
        name="block_back",
    )(z_array, left, *weights)


def reverse_kernel(layouts, count, z_ref, *refs):
    rows, refs = refs[:8], refs[8:]
    weights, refs = refs[:count], refs[count:]
    fronts, backs = [bind(layout, weights) for layout in layouts]
    slope_ref, qkv_ref, log_ref, table_ref, mask_ref = refs[:5]
    left_ref, own_ref, other_ref, sums_ref, relative = refs[5:]
    take_rows(z_ref, rows, relative)
    grad = relative[...]
    table = get(table_ref, 0, 3 * PAIR)
    n = fronts[0][2] - fronts[0][1]
    ffn_n = n - 3 * PAIR
    for x in range(2):
        both = times_t(grad, backs, x)
        gate = both[:, PAIR:] * get(slope_ref, x * ffn_n, ffn_n).astype(F32)
        put(left_ref, x * n + 3 * PAIR, gate)
        queries, keys, values = [get(qkv_ref, (3 * x + which) * PAIR, PAIR) for which in range(3)]
        grads = attend_back(
            queries, keys, values, get(log_ref, x * PAIR, PAIR), both[:, :PAIR].astype(BF), mask_ref[0]
        )
        grads = [turn_back(grads[0] * HEAD_DIM**-0.5, table), turn_back(grads[1], table), grads[2]]
        for which, value in enumerate(grads):
            put(left_ref, x * n + which * PAIR, value)
    left = get(left_ref, 0, left_ref.shape[-1])
    put_parts(z_ref, times(left, fronts), own_ref, other_ref)
    sums = jnp.sum(left.astype(F32), 0, keepdims=True)

    @pl.when(pl.program_id(0) == 0)
    def _():
        sums_ref[...] = sums

    @pl.when(pl.program_id(0) > 0)
    def _():
        sums_ref[...] += sums


def reverse(z_array, rows, layouts, weights, slope, qkv, logs, table, mask):
    _, first, last = layouts[0][0]
    n = last - first
    return pl.pallas_call(
        lambda *refs: reverse_kernel(layouts, len(weights), *refs),
        grid=(ZS,),
        in_specs=[SMEM_SPEC]
        + [fixed(a.shape) for a in (*rows, *weights)]
        + [slot_spec(a.shape[-1]) for a in (slope, qkv, logs, table)]
        + [MASK_SPEC],
        out_specs=[slot_spec(2 * n), PART_SPEC, PART_SPEC]
        + [pl.BlockSpec((1, 2 * n), lambda k: (0, 0))],
        out_shape=[slot_shape(2 * n, BF), PART_SHAPE, PART_SHAPE]
        + [jax.ShapeDtypeStruct((1, 2 * n), F32)],
        scratch_shapes=[RELATIVE],
        compiler_params=pltpu.CompilerParams(vmem_limit_bytes=VMEM_LIMIT),
        cost_estimate=SMALL_COST,
        name="block_reverse",
    )(z_array, *rows, *weights, slope, qkv, logs, table, mask)


def centred(hidden):
    centre = hidden - jnp.mean(hidden, -1, keepdims=True)
    rstd = lax.rsqrt(jnp.mean(centre * centre, -1, keepdims=True) + NORM_EPS)
    return centre * rstd, rstd


def model_row(ref, layer, which):
    return ref[layer * 4 + which : layer * 4 + which + 1].astype(F32)


def add_parts(refs):
    total = refs[0][...]
    for ref in refs[1:]:
        total = total + ref[...].astype(F32)
    return total


def norm_kernel(layer, final, hidden_ref, *refs):
    hidden = hidden_ref[...].astype(F32)
    parts, (model_ref, *outs) = refs[: len(refs) - 2 - (not final)], refs[len(refs) - 2 - (not final) :]
    if parts:
        bias = model_row(model_ref, layer - 1, 2) + model_row(model_ref, layer - 1, 3)
        hidden = hidden + add_parts(parts) + bias
    outs[0][...] = hidden.astype(outs[0].dtype)
    if not final:
        xhat, _ = centred(hidden)
        outs[1][...] = (
            xhat * model_row(model_ref, layer, 0) + model_row(model_ref, layer, 1)
        ).astype(BF)


def norm(layer, final, hidden, parts, model_vec):
    shapes = [jax.ShapeDtypeStruct((HALF, D), kind) for kind in ((BF,) if final else (F32, BF))]
    return pl.pallas_call(
        lambda *refs: norm_kernel(layer, final, *refs),
        out_shape=shapes,
        compiler_params=pltpu.CompilerParams(vmem_limit_bytes=VMEM_LIMIT),
        cost_estimate=SMALL_COST,
        name="norm",
    )(hidden, *parts, model_vec)


def norm_back_kernel(layer, count, grad_ref, hidden_ref, *refs):
    parts, model_ref, (next_ref, low_ref, sums_ref) = refs[:count], refs[count], refs[-3:]
    grad_next = grad_ref[...].astype(F32)
    grad_normed = add_parts(parts)
    xhat, rstd = centred(hidden_ref[...].astype(F32))
    sums_ref[...] = jnp.concatenate(
        [
            jnp.sum(grad_normed * xhat, 0, keepdims=True),
            jnp.sum(grad_normed, 0, keepdims=True),
            jnp.sum(grad_next, 0, keepdims=True),
            jnp.zeros((5, grad_next.shape[1]), F32),
        ],
        0,
    )
    scaled = grad_normed * model_row(model_ref, layer, 0)
    grad = grad_next + rstd * (
        scaled
        - jnp.mean(scaled, -1, keepdims=True)
        - xhat * jnp.mean(scaled * xhat, -1, keepdims=True)
    )
    next_ref[...] = grad
    low_ref[...] = grad.astype(BF)


def norm_back(layer, grad_next, hidden, parts, model_vec, earlier=()):
    vmem = pl.BlockSpec(memory_space=pltpu.VMEM)
    return pl.pallas_call(
        lambda *refs: norm_back_kernel(layer, len(parts), *refs),
        in_specs=[vmem] * (3 + len(parts)) + [ANY_SPEC] * len(earlier),
        out_shape=[
            jax.ShapeDtypeStruct((HALF, D), F32),
            jax.ShapeDtypeStruct((HALF, D), BF),
            jax.ShapeDtypeStruct((8, D), F32),
        ],
        compiler_params=pltpu.CompilerParams(vmem_limit_bytes=VMEM_LIMIT),
        cost_estimate=SMALL_COST,
        name="norm_back",
    )(grad_next, hidden, *parts, model_vec, *earlier)


def fold_kernel(count, z_ref, own_ref, other_ref, *refs):
    outs = refs[len(refs) - count :]
    totals = [own_ref[k].astype(F32) + other_ref[k].astype(F32) for k in range(ZS)]
    for k in range(ZS):
        outs[k][...] = totals[k].astype(outs[k].dtype)
    if len(outs) > ZS:
        outs[ZS][...] = jnp.where(z_ref[0] == 0, totals[1], totals[3]).astype(BF)


def fold(z_array, own, other, kinds, earlier=()):
    return pl.pallas_call(
        lambda *refs: fold_kernel(len(kinds), *refs),
        in_specs=[pl.BlockSpec(memory_space=pltpu.SMEM)]
        + [pl.BlockSpec(memory_space=pltpu.VMEM)] * 2
        + [ANY_SPEC] * len(earlier),
        out_shape=[jax.ShapeDtypeStruct((HALF, D), kind) for kind in kinds],
        compiler_params=pltpu.CompilerParams(vmem_limit_bytes=VMEM_LIMIT),
        cost_estimate=SMALL_COST,
        name="fold",
    )(z_array, own, other, *earlier)


class Place:
    def __init__(self, ny):
        self.ny = ny
        self.z = lax.axis_index("z")
        self.y = lax.axis_index("y")
        self.x = lax.axis_index("x")
        self.c = lax.axis_index("c")

    def own_first(self, lower, upper, index, axis):
        mine = jnp.where(index == 0, lower, upper)
        other = jnp.where(index == 0, upper, lower)
        return jnp.concatenate([mine, other], axis)

    def to_local(self, array):
        parts = array.reshape(*array.shape[:-1], ZS, self.ny, -1)
        parts = jnp.swapaxes(parts, -2, -3).reshape(*array.shape[:-1], 2, -1)
        lower, upper = parts[..., 0, :], parts[..., 1, :]
        if self.ny == 2:
            return self.own_first(lower, upper, self.y, -1)
        return jnp.concatenate([lower, upper], -1)

    def from_local(self, array):
        half = array.shape[-1] // 2
        lower, upper = array[..., :half], array[..., half:]
        if self.ny == 2:
            array = self.own_first(lower, upper, self.y, -1)
        parts = array.reshape(*array.shape[:-1], self.ny, ZS, -1)
        return jnp.swapaxes(parts, -2, -3).reshape(*array.shape)

    def y_columns(self, array):
        if self.ny == 2:
            return jnp.concatenate([array, swap(array, "y")], -1)
        return lax.all_gather(array, "y", axis=array.ndim - 1, tiled=True)

    def y_place(self, array):
        if self.ny == 2:
            other = swap(array, "y")
            return self.own_first(array, other, self.y, -1)
        return lax.all_gather(array, "y", axis=array.ndim - 1, tiled=True)


def after(array, *earlier):
    return lax.optimization_barrier((array, *earlier))[0]


def gather_z(array):
    return [array] + [shift_z(array, k) for k in range(1, ZS)]


def line_z(array, pairs):
    return lax.ppermute(array, "z", pairs)


def gather_rows(rows, *earlier):
    mine = gather_z(rows)
    return mine + [swap(after(part, *earlier) if earlier else part, "c") for part in mine]


def gather_line(place, rows, *deadlines, second=()):
    far = swap(rows, "c")
    up_one = line_z(rows, [(0, 1), (1, 2), (2, 3)])
    down_one = line_z(rows, [(3, 2), (2, 1), (1, 0)])
    up_one, down_one = after(up_one, far, *second), after(down_one, *second)
    up_two = line_z(up_one, [(1, 2), (2, 3)])
    down_two = line_z(down_one, [(2, 1), (1, 0)])
    two = up_two + down_two
    if deadlines:
        two = after(two, *deadlines)
    far_two = swap(two, "c")
    end = after(line_z(two, [(2, 3), (1, 0)]), far_two)
    one = jnp.where(place.z == 0, end, up_one)
    three = jnp.where(place.z == ZS - 1, end, down_one)
    return [rows, one, two, three, far, swap(one, "c"), far_two, swap(three, "c")]


def scatter_rows(z_array, parts, *earlier):
    own, other = parts
    if earlier:
        other = after(other, *earlier)
    terms = fold(z_array, own, swap(other, "c"), (F32, BF, BF, BF))
    return [terms[0]] + [shift_z(terms[k], -k) for k in range(1, ZS)]


def scatter_line(z_array, parts, first=(), then=(), mid=(), last=(), tokens=()):
    own, other = parts
    if first:
        other = after(other, *first)
    other = swap(other, "c")
    if then:
        other = after(other, *then)
    own, one, two, three, end = fold(z_array, own, other, (F32, F32, F32, F32, BF), tokens)
    end = line_z(end, [(0, 1), (3, 2)])
    two = (two + end.astype(F32)).astype(BF)
    if mid:
        two = after(two, *mid)
    down_two = line_z(two, [(2, 1), (3, 2)])
    up_two = line_z(two, [(1, 2), (0, 1)])
    one = (one + down_two.astype(F32)).astype(BF)
    three = (three + up_two.astype(F32)).astype(BF)
    if last:
        one, three = after(one, *last), after(three, *last)
    down_one = line_z(one, [(1, 0), (2, 1), (3, 2)])
    up_one = line_z(three, [(0, 1), (1, 2), (2, 3)])
    return [own, down_one, up_one]


def whole_spec(shape):
    return pl.BlockSpec(shape, lambda *_: (0,) * len(shape))


def quarter(z_ref, k, sign):
    return (z_ref[0] + sign * k + ZS) % ZS


def weight_specs(kind, layer, dd, heads_n, ffn_n, sign):
    fronts = [
        pl.BlockSpec((1, 3, dd, heads_n), lambda k, z: (layer, 0, 0, quarter(z, k, sign))),
        pl.BlockSpec((1, dd, ffn_n), lambda k, z: (layer, 0, quarter(z, k, sign))),
    ]
    backs = [
        pl.BlockSpec((1, heads_n, dd), lambda k, z: (layer, quarter(z, k, sign), 0)),
        pl.BlockSpec((1, ffn_n, dd), lambda k, z: (layer, quarter(z, k, sign), 0)),
    ]
    return {"front": fronts, "back": backs, "both": fronts + backs}[kind]


def pack_kernel(kind, z_ref, *refs):
    refs, outs = refs[:-ZS], refs[-ZS:]
    parts = []
    if kind != "back":
        parts += [refs[0][0, which].T for which in range(3)] + [refs[1][0].T]
    if kind != "front":
        parts += [refs[-2][0], refs[-1][0]]
    block = jnp.concatenate(parts, 0).astype(BF)
    for k in range(ZS):

        @pl.when(pl.program_id(0) == k)
        def _():
            outs[k][...] = block


def pack(kind, layer, z_array, arrays, dd, heads_n, ffn_n):
    n = {"front": 3 * heads_n + ffn_n, "back": heads_n + ffn_n, "both": 4 * heads_n + 2 * ffn_n}[kind]
    return pl.pallas_call(
        lambda *refs: pack_kernel(kind, *refs),
        grid_spec=pltpu.PrefetchScalarGridSpec(
            num_scalar_prefetch=1,
            grid=(ZS,),
            in_specs=weight_specs(kind, layer, dd, heads_n, ffn_n, 1),
            out_specs=[whole_spec((n, dd))] * ZS,
        ),
        out_shape=[jax.ShapeDtypeStruct((n, dd), BF)] * ZS,
        compiler_params=pltpu.CompilerParams(vmem_limit_bytes=VMEM_LIMIT),
        cost_estimate=pl.CostEstimate(
            flops=0, bytes_accessed=6 * ZS * n * dd, transcendentals=0
        ),
        name="pack_" + kind,
    )(z_array, *arrays)


def stack_kernel(*refs):
    dd = refs[0].shape[1]
    for at, ref in enumerate(refs[:-1]):
        refs[-1][:, at * dd : (at + 1) * dd] = ref[...]


def stack(pieces):
    n, dd = pieces[0].shape
    if dd % 128:
        return jnp.concatenate(pieces, 1)
    return pl.pallas_call(
        stack_kernel,
        out_shape=jax.ShapeDtypeStruct((n, len(pieces) * dd), BF),
        compiler_params=pltpu.CompilerParams(vmem_limit_bytes=VMEM_LIMIT),
        cost_estimate=SMALL_COST,
        name="stack",
    )(*pieces)


def stack_rows_kernel(*refs):
    for at, ref in enumerate(refs[:-1]):
        refs[-1][at * HALF : (at + 1) * HALF] = ref[...]


def stack_rows(rows):
    return pl.pallas_call(
        stack_rows_kernel,
        out_shape=jax.ShapeDtypeStruct((len(rows) * HALF, D), BF),
        compiler_params=pltpu.CompilerParams(vmem_limit_bytes=VMEM_LIMIT),
        cost_estimate=SMALL_COST,
        name="stack_rows",
    )(*rows)


def spread_xy(kind, near, *earlier):
    cut = cut_of(kind)
    on_x, on_y = swap(near, "x"), swap(near, "y")
    one, two = on_x[:cut], on_y[cut:]
    if earlier:
        one, two = after(one, *earlier), after(two, *earlier)
    return near, on_y, on_x, swap(one, "y"), swap(two, "x")


def weight_grads(kind, left, right, cut):
    n, half = left.shape[1] // 2, right.shape[1] // 2
    cut = min(cut, n)
    lower, upper = right[:, :half], right[:, half:]
    own, other = left[:, :n], left[:, n:]
    return [
        dot_tn(one, two).astype(BF) if one.shape[1] else jnp.zeros((0, half), BF)
        for one, two in (
            (other[:, :cut], upper),
            (other[:, cut:], upper),
            (own, upper),
            (other, lower),
            (own, lower),
        )
    ]


def bump_kernel(count, *refs):
    parts, (one_ref, two_ref), (y_ref, x_ref) = refs[: 2 * count], refs[2 * count :][:2], refs[-2:]
    at = 0
    for on_y, on_x in zip(parts[:count], parts[count:]):
        rows = slice(at, at + on_y.shape[0])
        y_ref[rows] = on_y[...]
        x_ref[rows] = on_x[...]
        at += on_y.shape[0]
    cut = one_ref.shape[0]
    y_ref[:cut] = add_low(y_ref[:cut], one_ref[...])
    x_ref[cut:] = add_low(x_ref[cut:], two_ref[...])


def bump(on_y, on_x, far_one, far_two, earlier=()):
    n = sum(part.shape[0] for part in on_y)
    vmem = pl.BlockSpec(memory_space=pltpu.VMEM)
    return pl.pallas_call(
        lambda *refs: bump_kernel(len(on_y), *refs),
        in_specs=[vmem] * (2 * len(on_y) + 2) + [ANY_SPEC] * len(earlier),
        out_shape=[jax.ShapeDtypeStruct((n, on_y[0].shape[1]), BF)] * 2,
        compiler_params=pltpu.CompilerParams(vmem_limit_bytes=VMEM_LIMIT),
        cost_estimate=SMALL_COST,
        name="bump",
    )(*on_y, *on_x, far_one, far_two, *earlier)


def split_kernel(count, z_ref, *refs):
    near, (y_ref, x_ref, *_), outs = refs[:count], refs[count:], refs[-ZS:]
    value = jnp.concatenate([part[...] for part in near], 0).astype(F32)
    value = (value + y_ref[...].astype(F32) + x_ref[...].astype(F32)).astype(BF)
    for k in range(ZS):

        @pl.when(pl.program_id(0) == k)
        def _():
            outs[k][...] = value


def split(z_array, near, from_y, from_x, earlier=()):
    n, width = from_y.shape
    dd = width // ZS
    return pl.pallas_call(
        lambda *refs: split_kernel(len(near), *refs),
        grid_spec=pltpu.PrefetchScalarGridSpec(
            num_scalar_prefetch=1,
            grid=(ZS,),
            in_specs=[
                pl.BlockSpec((part.shape[0], dd), lambda k, z: (0, quarter(z, k, 1)))
                for part in (*near, from_y, from_x)
            ]
            + [ANY_SPEC] * len(earlier),
            out_specs=[whole_spec((n, dd))] * ZS,
        ),
        out_shape=[jax.ShapeDtypeStruct((n, dd), BF)] * ZS,
        compiler_params=pltpu.CompilerParams(vmem_limit_bytes=VMEM_LIMIT),
        cost_estimate=SMALL_COST,
        name="split",
    )(z_array, *near, from_y, from_x, *earlier)


def add_low(left, right):
    return (left.astype(F32) + right.astype(F32)).astype(BF)


def sum_plain(place, grads):
    own = jnp.concatenate([jnp.concatenate([g[4], g[2]], 1) for g in grads], 0)
    other = [jnp.concatenate([g[3], jnp.concatenate([g[0], g[1]], 0)], 1) for g in grads]
    both = add_low(own, swap(jnp.concatenate(other, 0), "x"))
    total = lax.psum_scatter(both, "y", scatter_dimension=1, tiled=True)
    n, width = total.shape
    dd = width // ZS
    return [lax.dynamic_slice(total, (0, (place.z + k) % ZS * dd), (n, dd)) for k in range(ZS)]


def adam_kernel(kind, heads_n, ffn_n, offset, rates, z_ref, *refs):
    pieces, states, outs = refs[:ZS], refs[ZS : ZS + 6], refs[-9:-1]
    refs[-1][...] = jnp.zeros_like(refs[-1])
    for k in range(ZS):

        @pl.when(pl.program_id(0) == k)
        def _():
            split = (3 if kind == "front" else 1) * heads_n
            piece = pieces[k][offset : offset + split + ffn_n]
            if kind == "front":
                grads = [
                    jnp.stack(
                        [
                            piece[which * heads_n : (which + 1) * heads_n].astype(F32).T
                            for which in range(3)
                        ]
                    )[None],
                    piece[split:].astype(F32).T[None],
                ]
            else:
                grads = [piece[:split].astype(F32)[None], piece[split:].astype(F32)[None]]
            for at, grad in enumerate(grads):
                weight, first, second = [ref[...] for ref in states[at * 3 : at * 3 + 3]]
                outs[at * 4][...] = grad
                new = adamw(weight, grad, first, second, rates[at], DECAY)
                for ref, value in zip(outs[at * 4 + 1 : at * 4 + 4], new):
                    ref[...] = value


def adam(kind, layer, z_array, pieces, offset, states, rates, earlier, tokens, heads_n, ffn_n):
    n, dd = pieces[0].shape
    first, second = weight_specs(kind, layer, dd, heads_n, ffn_n, -1)
    shapes = [jax.ShapeDtypeStruct(states[at].shape, F32) for at in (0, 3) for _ in range(4)]
    earlier = list(earlier or [])
    return pl.pallas_call(
        lambda *refs: adam_kernel(kind, heads_n, ffn_n, offset, rates, *refs),
        grid_spec=pltpu.PrefetchScalarGridSpec(
            num_scalar_prefetch=1,
            grid=(ZS,),
            in_specs=[whole_spec((n, dd))] * ZS
            + [first] * 3
            + [second] * 3
            + [ANY_SPEC] * (len(earlier) + len(tokens)),
            out_specs=[first] * 4 + [second] * 4 + [whole_spec((8, 128))],
        ),
        out_shape=shapes + [jax.ShapeDtypeStruct((8, 128), F32)],
        input_output_aliases={1 + ZS + 6 + at: at for at in range(len(earlier))},
        compiler_params=pltpu.CompilerParams(vmem_limit_bytes=VMEM_LIMIT),
        cost_estimate=SMALL_COST,
        name="adam_" + kind,
    )(z_array, *pieces, *states, *earlier, *tokens)


def tables(positions):
    half = ROT // 2
    places = jnp.maximum(positions, 0).astype(F32)
    frequency = 10000.0 ** (-(2.0 / ROT) * jnp.arange(half).astype(F32))
    angles = places[..., None] * frequency
    both = jnp.concatenate([jnp.cos(angles), jnp.sin(angles)], -1)
    pick = np.zeros((ROT, 3, 2, HEAD_DIM), np.float32)
    for at in range(half):
        pick[at, 0, :, at] = pick[at, 0, :, half + at] = 1.0
        pick[half + at, 1, :, at] = -1.0
        pick[half + at, 2, :, half + at] = 1.0
    rest = np.zeros((3, 2, HEAD_DIM), np.float32)
    rest[0, :, ROT:] = 1.0
    table = jnp.dot(both, pick.reshape(ROT, -1), precision=lax.Precision.HIGHEST)
    return table + rest.reshape(-1)


def adamw(weight, grad, first, second, rate, decay):
    first_new = BETA_ONE * first + (1.0 - BETA_ONE) * grad
    second_new = BETA_TWO * second + (1.0 - BETA_TWO) * grad * grad
    first_hat = first_new / (1.0 - BETA_ONE**STEP)
    second_hat = second_new / (1.0 - BETA_TWO**STEP)
    weight_new = weight - rate * (first_hat / (jnp.sqrt(second_hat) + ADAM_EPS) + decay * weight)
    return (first_new, second_new, weight_new)


def source_lane(at, y):
    return (at % ZS) * 2 + (at // ZS + y) % 2


def take_kernel(place_ref, rows_ref, grads_ref, live_ref, start_ref, low_ref):
    dd = D // (2 * ZS)
    for at in range(2 * ZS):
        lanes = pl.ds(pl.multiple_of(source_lane(at, place_ref[1]) * dd, 128), dd)
        to = slice(at * dd, (at + 1) * dd)
        start_ref[:, to] = rows_ref[:, lanes]
        low_ref[:, to] = (grads_ref[:, lanes].astype(F32) * live_ref[...]).astype(BF)


def take(place, activations, cotangent, live):
    m = place.x * 2 + place.c
    if place.ny != 2:
        mine = [
            place.to_local(lax.dynamic_slice_in_dim(array, m * HALF, HALF, 0))
            for array in (activations, cotangent)
        ]
        return mine[0], (mine[1].astype(F32) * live).astype(BF)
    where = jnp.stack([m, place.y]).astype(jnp.int32)
    return pl.pallas_call(
        take_kernel,
        grid_spec=pltpu.PrefetchScalarGridSpec(
            num_scalar_prefetch=1,
            grid=(1,),
            in_specs=[pl.BlockSpec((HALF, D), lambda at, ref: (ref[0], 0))] * 2
            + [pl.BlockSpec((HALF, 1), lambda at, ref: (0, 0))],
            out_specs=[pl.BlockSpec((HALF, D), lambda at, ref: (0, 0))] * 2,
        ),
        out_shape=[jax.ShapeDtypeStruct((HALF, D), BF)] * 2,
        cost_estimate=pl.CostEstimate(flops=0, bytes_accessed=8 * HALF * D, transcendentals=0),
        name="take",
    )(where, activations, cotangent, live)


def give_kernel(place_ref, *refs):
    dd = D // (2 * ZS)
    for block in range(4):

        @pl.when(pl.program_id(0) == block)
        def _():
            for at in range(2 * ZS):
                lanes = pl.ds(pl.multiple_of(source_lane(at, place_ref[2]) * dd, 128), dd)
                refs[-1][:, lanes] = refs[block][:, at * dd : (at + 1) * dd].astype(F32)


def give(place, blocks):
    where = jnp.stack([place.x, place.c, place.y]).astype(jnp.int32)
    if place.ny != 2:
        result = jnp.zeros((4 * HALF, D), F32)
        for at, block in enumerate(blocks):
            row = ((place.x + at // 2) % 2) * 2 + (place.c + at % 2) % 2
            result = lax.dynamic_update_slice(
                result, place.from_local(block).astype(F32), (row * HALF, 0)
            )
        return result

    def target(at, ref):
        return (((ref[0] + at // 2) % 2) * 2 + (ref[1] + at % 2) % 2, 0)

    return pl.pallas_call(
        give_kernel,
        grid_spec=pltpu.PrefetchScalarGridSpec(
            num_scalar_prefetch=1,
            grid=(4,),
            in_specs=[whole_spec((HALF, D))] * 4,
            out_specs=pl.BlockSpec((HALF, D), target),
        ),
        out_shape=jax.ShapeDtypeStruct((4 * HALF, D), F32),
        compiler_params=pltpu.CompilerParams(vmem_limit_bytes=VMEM_LIMIT),
        cost_estimate=SMALL_COST,
        name="give",
    )(where, *blocks)


def per_device(
    ny,
    activations,
    cotangent,
    positions,
    w_qkv,
    w_out,
    w_up,
    w_down,
    vec_model,
    vec_head,
    vec_ffn,
    first_qkv,
    first_out,
    first_up,
    first_down,
    first_model,
    first_head,
    first_ffn,
    second_qkv,
    second_out,
    second_up,
    second_down,
    second_model,
    second_head,
    second_ffn,
):
    place = Place(ny)
    dd = w_up.shape[1]
    heads_n = w_qkv.shape[3] // ZS
    ffn_n = w_up.shape[2] // ZS
    sizes = (dd, heads_n, ffn_n)
    z_array = place.z.reshape(1).astype(jnp.int32)

    model_own = vec_model.astype(BF).reshape(LAYERS * 4, dd)
    head_own, ffn_own = vec_head.astype(BF), vec_ffn.astype(BF)
    if ny == 2:
        first = jnp.concatenate(
            [model_own.reshape(-1), head_own.reshape(-1), ffn_own.reshape(-1)]
        )
        far = swap(first, "y")
        ends = [model_own.size, model_own.size + head_own.size, first.size]
        model_far, head_far, ffn_far = [
            far[start:end].reshape(own.shape)
            for start, end, own in zip([0] + ends, ends, (model_own, head_own, ffn_own))
        ]
        model_y = jnp.stack([model_own, model_far], 1)
        head_y = place.own_first(head_own, head_far, place.y, -1)
        ffn_y = place.own_first(ffn_own, ffn_far, place.y, -1)
    else:
        model_y = lax.all_gather(model_own, "y", axis=1)
        head_y = lax.all_gather(head_own, "y", axis=2, tiled=True)
        ffn_y = lax.all_gather(ffn_own, "y", axis=1, tiled=True)
    slim = jnp.concatenate([head_y.reshape(LAYERS, -1), ffn_y], 1)
    places_x = lax.dynamic_slice_in_dim(positions, place.x * ROWS, ROWS)
    places_x = place.own_first(places_x[:HALF], places_x[HALF:], place.c, 0)
    if ny == 2:
        pieces_front = pack("front", 0, z_array, (w_qkv, w_up), *sizes)
        slim = after(slim, *pieces_front)
    mine = jnp.concatenate([model_y.reshape(-1), places_x.astype(BF)])
    slim_x = swap(slim, "x")
    bias = jnp.concatenate([slim, slim_x], 1).astype(F32)
    packed = jnp.stack(
        [mine] + [lax.ppermute(mine, "z", [(i, i ^ k) for i in range(ZS)]) for k in range(1, ZS)]
    )
    if ny == 2:
        pieces_front = [after(piece, packed, slim_x) for piece in pieces_front]
        came_front = [pieces_front[0]] + [shift_z(pieces_front[k], k) for k in range(1, ZS)]
        on_x, on_y = swap(pieces_front[0], "x"), swap(pieces_front[0], "y")
        later_z = after(z_array, on_x, on_y)
        pieces_next = pack("both", 1, later_z, (w_qkv, w_up, w_out, w_down), *sizes)
        pieces_back = pack("back", 0, later_z, (w_out, w_down), *sizes)
        cut = cut_of("front")
        ready = *pieces_next, *pieces_back
        far_one, far_two = after(on_x[:cut], *ready), after(on_y[cut:], *ready)
        own_front = pieces_front[0], on_y, on_x, swap(far_one, "y"), swap(far_two, "x")
    everyone = jnp.arange(ZS, dtype=jnp.int32)
    by_z = jnp.take(packed, everyone ^ place.z, axis=0)
    model_vec = by_z[:, : LAYERS * 4 * ny * dd].reshape(ZS, LAYERS * 4, ny, dd)
    model_vec = model_vec.transpose(1, 2, 0, 3).reshape(LAYERS * 4, D)
    places = jnp.take(by_z[:, LAYERS * 4 * ny * dd :], (place.z - everyone) % ZS, axis=0)
    places = places.astype(F32).astype(jnp.int32)

    order = (jnp.arange(ROWS, dtype=jnp.int32) + place.c * HALF) % ROWS
    starts = order - jnp.maximum(places, 0)
    seen = (order[None, None, :] <= order[None, :, None]) & (
        order[None, None, :] >= starts[:, :, None]
    )
    mask = jnp.where(seen, 0.0, MASKED).astype(F32)
    table = tables(jnp.swapaxes(places.reshape(ZS, 2, HALF), 0, 1))

    mine = place.x * ROWS + place.c * HALF
    live = (lax.dynamic_slice_in_dim(positions, mine, HALF) >= 0).astype(F32)[:, None]
    if ny == 2:
        live = after(live, *own_front[1:3])
    start, last_low = take(place, activations, cotangent, live)

    kernel_z = z_array if ny == 2 else jnp.zeros_like(z_array)
    n_front, n_back = 3 * heads_n + ffn_n, heads_n + ffn_n
    n_both = n_front + n_back
    arrays = {"front": (w_qkv, w_up), "back": (w_out, w_down), "both": (w_qkv, w_up, w_out, w_down)}

    def packed_pieces(kind, layer):
        return pack(kind, layer, z_array, arrays[kind], *sizes)

    def send_z(pieces, *earlier):
        if earlier:
            pieces = [pieces[0]] + [after(piece, *earlier) for piece in pieces[1:]]
        return [pieces[0]] + [shift_z(pieces[k], k) for k in range(1, ZS)]

    def spread_plain(kind, layer):
        pieces = send_z(packed_pieces(kind, layer))
        n = pieces[0].shape[0]
        joined = jnp.zeros((n, ZS * dd), BF)
        for k, piece in enumerate(pieces):
            joined = lax.dynamic_update_slice(joined, piece, (0, (place.z - k) % ZS * dd))
        own = place.y_columns(joined).reshape(n, 2, ZS, -1)
        own = jnp.concatenate([own[:, :, :1], own[:, :, :0:-1]], 2).reshape(n, D)
        other = swap(own, "x")
        cut, half = cut_of(kind), D // 2
        return own[:, :half], own[:, half:], other[:, :half], other[:cut, half:], other[cut:, half:]

    def layout_of(kind, chunks, first=0):
        n, cut = {"front": n_front, "back": n_back}[kind], cut_of(kind)
        ids = [tuple(5 * c + at for c in range(chunks)) for at in range(5)]
        far = [(ids[3], 0, cut), (ids[4], 0, n - cut)]
        return (*((ids[at], 0, n) for at in range(3)), far)

    both_cut = cut_of("both")
    ids = [(at,) for at in range(5)]
    merged = (
        (*((ids[at], 0, n_front) for at in range(3)), [(ids[3], 0, both_cut), (ids[4], 0, n_front - both_cut)]),
        (*((ids[at], n_front, n_both) for at in range(3)), [(ids[4], n_front - both_cut, n_both - both_cut)]),
    )

    hidden, normed = norm(0, False, start, (), model_vec)
    if ny == 2:
        came_front[1] = after(came_front[1], start)
        came_back = send_z(pieces_back, *came_front[1:])
        rest_front = list(
            spread_xy("front", stack([after(came_front[1], *own_front[3:]), *came_front[2:]]))
        )
        fronts = [*own_front, *rest_front]
        rest_front[1] = after(rest_front[1], table, mask)
        near_back = stack([came_back[0], after(came_back[1], *rest_front[3:]), *came_back[2:]])
        on_x, on_y = swap(near_back, "x"), swap(near_back, "y")
        rows = gather_line(
            place, after(normed, *came_back[1:]), near_back, second=rest_front[1:3]
        )
        came_next = send_z(pieces_next, *rows[1:4])
    else:
        rows = gather_line(place, normed)
        fronts = spread_plain("front", 0)
        backs = spread_plain("back", 0)
    layouts = layout_of("front", 2 if ny == 2 else 1), layout_of("back", 1)
    shift = len(fronts)
    move = lambda part: (tuple(at + shift for at in part[0]), *part[1:])
    joint = layouts[0], (*map(move, layouts[1][:3]), [move(part) for part in layouts[1][3]])

    normed, qkv, logs, left, slope = front(
        kernel_z, rows, layouts[:1], fronts, bias[0:1], table, mask
    )
    kept = [(hidden, normed, qkv, logs, left, slope)]
    if ny == 2:
        cut, ready = cut_of("back"), (left, came_next[1], came_next[3])
        far_one, far_two = after(on_x[:cut], *ready), after(on_y[cut:], *ready)
        backs = near_back, on_y, on_x, swap(far_one, "y"), swap(far_two, "x")
    own, other = back(kernel_z, left, layouts[1], backs)
    if ny == 2:
        near_next = stack([came_next[0], after(came_next[1], other), *came_next[2:]])
        spread = spread_xy("both", near_next)
        parts = scatter_line(z_array, (own, other), first=(near_next,))
        parts[2] = after(parts[2], *spread[1:3])
    else:
        spread = spread_plain("both", 1)
        parts = scatter_line(z_array, (own, other))
    hidden, normed = norm(1, False, hidden, parts, model_vec)
    if ny == 2:
        rows = gather_line(place, normed)
    else:
        rows = gather_line(place, normed)
    mine_z = rows[1:4]
    normed, qkv, logs, left, slope, own, other = front(
        kernel_z, rows, merged, spread, bias[1:2], table, mask
    )
    kept.append((hidden, normed, qkv, logs, left, slope))
    rows = gather_rows(after(last_low, *mine_z))
    rest = scatter_rows(z_array, (own, other), *rows[1:4])
    rows[4] = after(rows[4], rest[0])

    outs = {"front": None, "back": None}
    states = {
        "front": (w_qkv, first_qkv, second_qkv, w_up, first_up, second_up),
        "back": (w_out, first_out, second_out, w_down, first_down, second_down),
    }
    rate_in = 3.0 / math.sqrt(D)
    rates = {
        "front": (rate_in, rate_in),
        "back": (12.0 / math.sqrt(D), 3.0 / math.sqrt(FF)),
    }

    def flat(array):
        return array.reshape(ALL_ROWS, -1)

    def first_hop(grads, earlier=()):
        far_one = jnp.concatenate([g[0] for g in grads], 0) if len(grads) > 1 else grads[0][0]
        far_two = jnp.concatenate([g[1] for g in grads], 0) if len(grads) > 1 else grads[0][1]
        return bump(
            [g[2] for g in grads],
            [g[3] for g in grads],
            swap(far_one, "x"),
            swap(far_two, "y"),
            earlier,
        )

    def second_hop(on_y, on_x):
        return swap(on_y, "y"), swap(on_x, "x")

    def step(kind, layer, pieces, offset, tokens=()):
        *outs[kind], token = adam(
            kind, layer, z_array, pieces, offset, states[kind], rates[kind], outs[kind], tokens, heads_n, ffn_n
        )
        return token

    sums, slims = {}, {}
    hidden_in, normed, qkv, logs, left, slope = kept[1]
    left_grad, own, other, slims[1] = reverse(
        kernel_z, rows, merged, spread, slope, qkv, logs, table, mask
    )
    grads = [
        weight_grads("back", flat(left), stack_rows(rows), cut_of("back")),
        weight_grads("front", flat(left_grad), flat(normed), cut_of("front")),
    ]
    (result,) = norm(LAYERS, True, hidden, rest, model_vec)
    result_x = swap(result, "x")
    results = [result, swap(result, "c"), result_x, swap(result_x, "c")]
    if ny == 2:
        hops = [first_hop(grads[:1])]
        seconds = [second_hop(*hops[0])]
        parts = scatter_line(z_array, (own, other), rest[1:], last=(*hops[0], result_x))
        late_far = [after(part, *seconds[0], *parts[1:]) for part in grads[1][:2]]
        hops.append(first_hop([late_far + grads[1][2:]]))
        grad_next, low, sums[1] = norm_back(1, last_low, hidden_in, parts, model_vec)
        seconds.append(second_hop(*hops[1]))
        rows = gather_line(place, low, *hops[1], second=(results[1], results[3]))
        came_one = [send_z(split(z_array, grads[0][4:], *seconds[0]), *rows[5:]), None]
    else:
        parts = scatter_line(z_array, (own, other))
        grad_next, low, sums[1] = norm_back(1, last_low, hidden_in, parts, model_vec)
        rows = gather_line(place, low)
        came_one = [send_z(sum_plain(place, grads[:1])), sum_plain(place, grads[1:])]
    hidden_in, normed, qkv, logs, left, slope = kept[0]
    left_grad, own, other, slims[0] = reverse(
        kernel_z, rows, joint, [*fronts, *backs], slope, qkv, logs, table, mask
    )
    left_grad = after(left_grad, *came_one[0][1:])
    if ny == 2:
        came_one[1] = split(z_array, grads[1][4:], *seconds[1], [slims[0]])
    grads_front = weight_grads("front", flat(left_grad), flat(normed), cut_of("front"))
    came_one[1] = send_z(came_one[1], *came_one[0][1:])
    if ny == 2:
        hop_front = first_hop([grads_front])
        second_front = second_hop(*hop_front)
        rows = [after(row, hop_front[0]) for row in rows]
    grads_back = weight_grads("back", flat(left), stack_rows(rows), cut_of("back"))
    tokens = [step("back", 1, came_one[0], 0), step("front", 1, came_one[1], 0)]
    result_rows = give(place, results)
    if ny == 2:
        parts = scatter_line(
            z_array,
            (own, other),
            (came_one[1][1], came_one[1][3], *hop_front),
            came_one[1][2:3],
            second_front,
        )
        near_front = after(grads_front[4], *grads_back[:2])
        sum_front = split(z_array, [near_front], *second_front)
        came_front = send_z(sum_front)
        late_far = [after(part, *second_front) for part in grads_back[:2]]
        hop_back = first_hop([late_far + grads_back[2:]])
        second_back = second_hop(*(after(p, came_front[1], came_front[3]) for p in hop_back))
        sum_back = split(z_array, grads_back[4:], *second_back)
        came_back = send_z(sum_back)
        norm_parts = [*parts[:2], after(parts[2], *came_front[1:], *second_back)]
    else:
        parts = scatter_line(z_array, (own, other))
        came_front = send_z(sum_plain(place, [grads_front]))
        sum_back = sum_plain(place, [grads_back])
        came_back = send_z(sum_back)
        norm_parts = parts
    grad_next, low, sums[0] = norm_back(
        0, grad_next, hidden_in, norm_parts, model_vec, [*tokens, result_rows]
    )
    came_front = [came_front[0], *(after(piece, sum_back[0]) for piece in came_front[1:])]
    token = step("front", 0, came_front, 0)
    step("back", 0, came_back, 0, [token])
    late = sum_back[0]

    low_x = swap(low, "x")
    low, low_x = [after(part, *came_back[1:]) for part in (low, low_x)]
    both = after(jnp.concatenate([slims[0], slims[1]], 0), late)
    n = both.shape[1] // 2
    slim = both[:, :n] + swap(both[:, n:], "x")
    heads = slim[:, : 3 * heads_n].reshape(LAYERS, 3, ny, -1)
    ffns = slim[:, 3 * heads_n :].reshape(LAYERS, ny, -1)
    slim = jnp.concatenate([heads.swapaxes(1, 2).reshape(LAYERS, ny, -1), ffns], 2)
    if ny == 2:
        mine, far = [jnp.where(place.y == at, slim[:, 0], slim[:, 1]) for at in range(2)]
        slim = mine + swap(far, "y")
    else:
        slim = lax.psum_scatter(slim, "y", scatter_dimension=1, tiled=False)
    at = 3 * heads_n // ny
    grad_head = slim[:, :at].reshape(LAYERS, 3, -1)
    grad_ffn = slim[:, at:]

    total = jnp.stack([sums[layer][:3] for layer in range(LAYERS)])
    total = total + swap(total, "x")
    total = total + swap(total, "c")
    if ny == 2:
        half = D // 2
        total = total[..., :half] + swap(total[..., half:], "y")
    else:
        total = lax.psum_scatter(total, "y", scatter_dimension=2, tiled=True)
    grad_model = lax.dynamic_slice_in_dim(total, place.z * dd, dd, 2)
    for k in range(1, ZS):
        grad_model = grad_model + shift_z(
            lax.dynamic_slice_in_dim(total, (place.z + k) % ZS * dd, dd, 2), k
        )
    grad_model = jnp.concatenate([grad_model, grad_model[:, 2:]], 1)

    small = []
    for weight, grad, first, second in (
        (vec_model, grad_model, first_model, second_model),
        (vec_head, grad_head, first_head, second_head),
        (vec_ffn, grad_ffn, first_ffn, second_ffn),
    ):
        small.append(grad)
        small.extend(adamw(weight, grad, first, second, 0.6, 0.0))
    ones, twos = outs["front"], outs["back"]
    return (
        result_rows,
        give(place, [low, swap(low, "c"), low_x, swap(low_x, "c")]),
        *ones[:4],
        *twos[:4],
        *ones[4:],
        *twos[4:],
        *small,
    )


def solution(mesh):
    n_dp, n_mp = mesh.devices.shape
    ny = n_dp // ZS
    split = Mesh(mesh.devices.reshape(ZS, ny, n_mp // 2, 2), ("z", "y", "x", "c"))
    dp, mp = ("z", "y"), ("x", "c")
    both = ("x", "c", "z", "y")
    params = (
        P(None, None, dp, mp),
        P(None, mp, dp),
        P(None, dp, mp),
        P(None, mp, dp),
        P(None, None, dp),
        P(None, None, both),
        P(None, both),
    )
    tokens = (P(dp, None), P(dp, None))
    return jax.shard_map(
        lambda *arrays: per_device(ny, *arrays),
        mesh=split,
        in_specs=(*tokens, P(dp), *params, *params, *params),
        out_specs=(*tokens, *(spec for spec in params for _ in range(4))),
        check_vma=False,
    )
```

```python
import math

import jax
import jax.numpy as jnp
import numpy as np
from jax import lax
from jax.experimental import pallas as pl
from jax.experimental.pallas import tpu as pltpu
from jax.sharding import Mesh
from jax.sharding import PartitionSpec as P

D = 2048
HEAD_DIM = 64
ROT = 32
FF = 8192
LAYERS = 2
STEP = 10
ROWS = 256
ZS = 4
HALF = 128
ORDER = (0, 1, 3, 2)
PAIR = 2 * HEAD_DIM

BETA_ONE = 0.9
BETA_TWO = 0.95
ADAM_EPS = 1e-08
DECAY = 0.1
NORM_EPS = 1e-05
MASKED = -1e30
BF = jnp.bfloat16
F32 = jnp.float32
VMEM_LIMIT = 58 * 2**20
SMALL_COST = pl.CostEstimate(flops=1024, bytes_accessed=1024, transcendentals=0)


def shift_z(array, step):
    return lax.ppermute(array, "z", [(i, (i + step) % ZS) for i in range(ZS)])


def swap(array, axis):
    return lax.ppermute(array, axis, [(0, 1), (1, 0)])


def dot_nt(left, right):
    return lax.dot_general(left, right, (((1,), (1,)), ((), ())), preferred_element_type=F32)


def dot_nn(left, right):
    return lax.dot_general(left, right, (((1,), (0,)), ((), ())), preferred_element_type=F32)


def dot_tn(left, right):
    return lax.dot_general(left, right, (((0,), (0,)), ((), ())), preferred_element_type=F32)


def turn(values, table):
    return (
        values * table[:, :PAIR]
        + pltpu.roll(values, PAIR - ROT // 2, 1) * table[:, PAIR : 2 * PAIR]
        + pltpu.roll(values, ROT // 2, 1) * table[:, 2 * PAIR :]
    )


def turn_back(grads, table):
    return (
        grads * table[:, :PAIR]
        - pltpu.roll(grads, PAIR - ROT // 2, 1) * table[:, PAIR : 2 * PAIR]
        - pltpu.roll(grads, ROT // 2, 1) * table[:, 2 * PAIR :]
    )


def low_lanes():
    return lax.broadcasted_iota(jnp.int32, (ROWS, PAIR), 1) < HEAD_DIM


def head_only(values, head):
    low_half = low_lanes()
    mine = low_half if head == 0 else jnp.logical_not(low_half)
    return jnp.where(mine, values, jnp.zeros_like(values))


def attend(queries, keys, values, mask):
    outs, logs = [], []
    for head in range(2):
        scores = dot_nt(head_only(queries, head), keys) + mask
        top = jnp.max(scores, -1, keepdims=True)
        exponent = jnp.exp(scores - top)
        total = jnp.sum(exponent, -1, keepdims=True)
        outs.append(dot_nn((exponent * (1.0 / total)).astype(BF), values))
        logs.append(jnp.broadcast_to(top + jnp.log(total), (ROWS, PAIR)))
    low_half = low_lanes()
    return jnp.where(low_half, *outs), jnp.where(low_half, *logs)


def attend_back(queries, keys, values, logs, grad, mask):
    grads = []
    for head in range(2):
        at = head * HEAD_DIM
        scores = dot_nt(head_only(queries, head), keys) + mask
        probs = jnp.exp(scores - logs[:, at : at + 1])
        grad_probs = dot_nt(head_only(grad, head), values)
        row_dot = jnp.sum(probs * grad_probs, -1, keepdims=True)
        grad_scores = (probs * (grad_probs - row_dot)).astype(BF)
        grads.append(
            (
                dot_nn(grad_scores, keys),
                dot_tn(grad_scores, queries),
                dot_tn(probs.astype(BF), grad),
            )
        )
    low_half = low_lanes()
    return [jnp.where(low_half, one, two) for one, two in zip(*grads)]


def cut_of(kind):
    return {"front": 3 * PAIR, "back": 2 * PAIR, "both": 6 * PAIR}[kind]


def nt_cols(left, segment):
    chunks, first, last = segment
    total, at = 0.0, 0
    for chunk in chunks:
        total = total + dot_nt(left[:, at : at + chunk.shape[1]], chunk[first:last])
        at += chunk.shape[1]
    return total


def nn_cols(left, segment):
    chunks, first, last = segment
    parts = [dot_nn(left, chunk[first:last]) for chunk in chunks]
    return parts[0] if len(parts) == 1 else jnp.concatenate(parts, 1)


def times_t(left, weights, x):
    near, on_y, on_x, far = weights
    half = left.shape[1] // 2
    lower, upper = left[:, :half], left[:, half:]
    if x == 0:
        return nt_cols(lower, near) + nt_cols(upper, on_y)
    parts = [nt_cols(upper, segment) for segment in far]
    return nt_cols(lower, on_x) + (parts[0] if len(parts) == 1 else jnp.concatenate(parts, 1))


def times(left, weights):
    near, on_y, on_x, far = weights
    n = near[2] - near[1]
    own, other = left[:, :n], left[:, n:]
    lower = nn_cols(own, near) + nn_cols(other, on_x)
    upper, at = nn_cols(own, on_y), 0
    for segment in far:
        rows = segment[2] - segment[1]
        upper = upper + nn_cols(other[:, at : at + rows], segment)
        at += rows
    return lower, upper


def bind(layout, refs):
    chunks = lambda part: (tuple(refs[at] for at in part[0]), part[1], part[2])
    near, on_y, on_x, far = layout
    return chunks(near), chunks(on_y), chunks(on_x), [chunks(part) for part in far]


def lanes_of(z_ref, k, y, dd):
    return pl.ds(pl.multiple_of(y * ZS * dd + (z_ref[0] - ORDER[k] + ZS) % ZS * dd, dd), dd)


def take_rows(z_ref, sources, relative, target=None):
    dd = relative.shape[1] // (2 * ZS)
    for slot in range(ZS):

        @pl.when(pl.program_id(0) == slot)
        def _():
            for core in range(2):
                source = sources[core * ZS + slot]
                rows = slice(core * HALF, (core + 1) * HALF)
                for y in range(2):
                    for k in range(ZS):
                        to = (y * ZS + k) * dd
                        relative[rows, to : to + dd] = source[:, lanes_of(z_ref, k, y, dd)]
                if target is not None:
                    target[core, 0] = source[...]


def put(ref, at, value):
    width = value.shape[1]
    ref[:, :, :, at : at + width] = value.astype(ref.dtype).reshape(2, 1, HALF, width)


def get(ref, at, width):
    return ref[:, :, :, at : at + width].reshape(ROWS, width)


def put_parts(z_ref, halves, own_ref, other_ref):
    for y, value in enumerate(halves):
        dd = value.shape[1] // ZS
        for k in range(ZS):
            lanes = lanes_of(z_ref, k, y, dd)
            part = value[:, k * dd : (k + 1) * dd].astype(BF)
            own_ref[0, :, lanes] = part[:HALF]
            other_ref[0, :, lanes] = part[HALF:]


def front_kernel(layouts, count, z_ref, *refs):
    rows, refs = refs[:8], refs[8:]
    weights, refs = refs[:count], refs[count:]
    fronts = bind(layouts[0], weights)
    bias_ref, table_ref, mask_ref, normed_ref, qkv_ref, log_ref, left_ref, slope_ref = refs[:8]
    relative = refs[-1]
    take_rows(z_ref, rows, relative, normed_ref)
    normed = relative[...]
    table = get(table_ref, 0, 3 * PAIR)
    n = fronts[0][2] - fronts[0][1]
    ffn_n = n - 3 * PAIR
    root = math.sqrt(2.0 / math.pi)
    for x in range(2):
        both = times_t(normed, fronts, x) + bias_ref[:, x * n : (x + 1) * n]
        gate = both[:, 3 * PAIR :]
        square = gate * gate
        bend = jnp.tanh(root * gate * (1.0 + 0.044715 * square))
        half_up = 0.5 + 0.5 * bend
        put(left_ref, x * (PAIR + ffn_n) + PAIR, gate * half_up)
        slope = half_up + (0.5 * gate) * (1.0 - bend * bend) * (
            root + (3.0 * 0.044715 * root) * square
        )
        put(slope_ref, x * ffn_n, slope)
        queries = turn(both[:, :PAIR], table).astype(BF) * jnp.asarray(HEAD_DIM**-0.5, BF)
        keys = turn(both[:, PAIR : 2 * PAIR], table).astype(BF)
        values = both[:, 2 * PAIR : 3 * PAIR].astype(BF)
        out, logs = attend(queries, keys, values, mask_ref[0])
        for which, value in enumerate((queries, keys, values)):
            put(qkv_ref, (3 * x + which) * PAIR, value)
        put(left_ref, x * (PAIR + ffn_n), out)
        put(log_ref, x * PAIR, logs)
    if len(layouts) > 1:
        backs = bind(layouts[1], weights)
        put_parts(z_ref, times(get(left_ref, 0, left_ref.shape[-1]), backs), *refs[8:10])


def slot_spec(width):
    return pl.BlockSpec((2, 1, HALF, width), lambda k: (0, k, 0, 0))


def fixed(shape):
    return pl.BlockSpec(
        shape, lambda *_: (0,) * len(shape), pipeline_mode=pl.Buffered(buffer_count=1)
    )


def slot_shape(width, kind):
    return jax.ShapeDtypeStruct((2, ZS, HALF, width), kind)


SMEM_SPEC = pl.BlockSpec(memory_space=pltpu.SMEM)
ANY_SPEC = pl.BlockSpec(memory_space=pl.ANY)
MASK_SPEC = pl.BlockSpec((1, ROWS, ROWS), lambda k: (k, 0, 0))
PART_SPEC = pl.BlockSpec((1, HALF, D), lambda k: (k, 0, 0))
PART_SHAPE = jax.ShapeDtypeStruct((ZS, HALF, D), BF)
ALL_ROWS = 2 * ZS * HALF
RELATIVE = pltpu.VMEM((ROWS, D), BF)


def front(z_array, rows, layouts, weights, bias, table, mask):
    n = bias.shape[1] // 2
    ffn_n = n - 3 * PAIR
    widths = [(D, BF), (6 * PAIR, BF), (2 * PAIR, F32), (2 * (PAIR + ffn_n), BF), (2 * ffn_n, BF)]
    parts = 2 * (len(layouts) - 1)
    return pl.pallas_call(
        lambda *refs: front_kernel(layouts, len(weights), *refs),
        grid=(ZS,),
        in_specs=[SMEM_SPEC]
        + [fixed(a.shape) for a in (*rows, *weights, bias)]
        + [slot_spec(3 * PAIR), MASK_SPEC],
        out_specs=[slot_spec(width) for width, _ in widths] + [PART_SPEC] * parts,
        out_shape=[slot_shape(*pair) for pair in widths] + [PART_SHAPE] * parts,
        scratch_shapes=[RELATIVE],
        compiler_params=pltpu.CompilerParams(vmem_limit_bytes=VMEM_LIMIT),
        cost_estimate=SMALL_COST,
        name="block_front",
    )(z_array, *rows, *weights, bias, table, mask)


def back_kernel(layout, z_ref, left_ref, *refs):
    left = get(left_ref, 0, left_ref.shape[-1])
    put_parts(z_ref, times(left, bind(layout, refs[:-2])), *refs[-2:])


def back(z_array, left, layout, weights):
    return pl.pallas_call(
        lambda *refs: back_kernel(layout, *refs),
        grid=(ZS,),
        in_specs=[SMEM_SPEC, slot_spec(left.shape[-1])] + [fixed(a.shape) for a in weights],
        out_specs=[PART_SPEC] * 2,
        out_shape=[PART_SHAPE] * 2,
        compiler_params=pltpu.CompilerParams(vmem_limit_bytes=VMEM_LIMIT),
        cost_estimate=SMALL_COST,
        name="block_back",
    )(z_array, left, *weights)


def reverse_kernel(layouts, count, z_ref, *refs):
    rows, refs = refs[:8], refs[8:]
    weights, refs = refs[:count], refs[count:]
    fronts, backs = [bind(layout, weights) for layout in layouts]
    slope_ref, qkv_ref, log_ref, table_ref, mask_ref = refs[:5]
    left_ref, own_ref, other_ref, sums_ref, relative = refs[5:]
    take_rows(z_ref, rows, relative)
    grad = relative[...]
    table = get(table_ref, 0, 3 * PAIR)
    n = fronts[0][2] - fronts[0][1]
    ffn_n = n - 3 * PAIR
    for x in range(2):
        both = times_t(grad, backs, x)
        gate = both[:, PAIR:] * get(slope_ref, x * ffn_n, ffn_n).astype(F32)
        put(left_ref, x * n + 3 * PAIR, gate)
        queries, keys, values = [get(qkv_ref, (3 * x + which) * PAIR, PAIR) for which in range(3)]
        grads = attend_back(
            queries, keys, values, get(log_ref, x * PAIR, PAIR), both[:, :PAIR].astype(BF), mask_ref[0]
        )
        grads = [turn_back(grads[0] * HEAD_DIM**-0.5, table), turn_back(grads[1], table), grads[2]]
        for which, value in enumerate(grads):
            put(left_ref, x * n + which * PAIR, value)
    left = get(left_ref, 0, left_ref.shape[-1])
    put_parts(z_ref, times(left, fronts), own_ref, other_ref)
    sums = jnp.sum(left.astype(F32), 0, keepdims=True)

    @pl.when(pl.program_id(0) == 0)
    def _():
        sums_ref[...] = sums

    @pl.when(pl.program_id(0) > 0)
    def _():
        sums_ref[...] += sums


def reverse(z_array, rows, layouts, weights, slope, qkv, logs, table, mask):
    _, first, last = layouts[0][0]
    n = last - first
    return pl.pallas_call(
        lambda *refs: reverse_kernel(layouts, len(weights), *refs),
        grid=(ZS,),
        in_specs=[SMEM_SPEC]
        + [fixed(a.shape) for a in (*rows, *weights)]
        + [slot_spec(a.shape[-1]) for a in (slope, qkv, logs, table)]
        + [MASK_SPEC],
        out_specs=[slot_spec(2 * n), PART_SPEC, PART_SPEC]
        + [pl.BlockSpec((1, 2 * n), lambda k: (0, 0))],
        out_shape=[slot_shape(2 * n, BF), PART_SHAPE, PART_SHAPE]
        + [jax.ShapeDtypeStruct((1, 2 * n), F32)],
        scratch_shapes=[RELATIVE],
        compiler_params=pltpu.CompilerParams(vmem_limit_bytes=VMEM_LIMIT),
        cost_estimate=SMALL_COST,
        name="block_reverse",
    )(z_array, *rows, *weights, slope, qkv, logs, table, mask)


def centred(hidden):
    centre = hidden - jnp.mean(hidden, -1, keepdims=True)
    rstd = lax.rsqrt(jnp.mean(centre * centre, -1, keepdims=True) + NORM_EPS)
    return centre * rstd, rstd


def model_row(ref, layer, which):
    return ref[layer * 4 + which : layer * 4 + which + 1].astype(F32)


def add_parts(refs):
    total = refs[0][...]
    for ref in refs[1:]:
        total = total + ref[...].astype(F32)
    return total


def norm_kernel(layer, final, hidden_ref, *refs):
    hidden = hidden_ref[...].astype(F32)
    parts, (model_ref, *outs) = refs[: len(refs) - 2 - (not final)], refs[len(refs) - 2 - (not final) :]
    if parts:
        bias = model_row(model_ref, layer - 1, 2) + model_row(model_ref, layer - 1, 3)
        hidden = hidden + add_parts(parts) + bias
    outs[0][...] = hidden.astype(outs[0].dtype)
    if not final:
        xhat, _ = centred(hidden)
        outs[1][...] = (
            xhat * model_row(model_ref, layer, 0) + model_row(model_ref, layer, 1)
        ).astype(BF)


def norm(layer, final, hidden, parts, model_vec):
    shapes = [jax.ShapeDtypeStruct((HALF, D), kind) for kind in ((BF,) if final else (F32, BF))]
    return pl.pallas_call(
        lambda *refs: norm_kernel(layer, final, *refs),
        out_shape=shapes,
        compiler_params=pltpu.CompilerParams(vmem_limit_bytes=VMEM_LIMIT),
        cost_estimate=SMALL_COST,
        name="norm",
    )(hidden, *parts, model_vec)


def norm_back_kernel(layer, count, grad_ref, hidden_ref, *refs):
    parts, model_ref, (next_ref, low_ref, sums_ref) = refs[:count], refs[count], refs[-3:]
    grad_next = grad_ref[...].astype(F32)
    grad_normed = add_parts(parts)
    xhat, rstd = centred(hidden_ref[...].astype(F32))
    sums_ref[...] = jnp.concatenate(
        [
            jnp.sum(grad_normed * xhat, 0, keepdims=True),
            jnp.sum(grad_normed, 0, keepdims=True),
            jnp.sum(grad_next, 0, keepdims=True),
            jnp.zeros((5, grad_next.shape[1]), F32),
        ],
        0,
    )
    scaled = grad_normed * model_row(model_ref, layer, 0)
    grad = grad_next + rstd * (
        scaled
        - jnp.mean(scaled, -1, keepdims=True)
        - xhat * jnp.mean(scaled * xhat, -1, keepdims=True)
    )
    next_ref[...] = grad
    low_ref[...] = grad.astype(BF)


def norm_back(layer, grad_next, hidden, parts, model_vec, earlier=()):
    vmem = pl.BlockSpec(memory_space=pltpu.VMEM)
    return pl.pallas_call(
        lambda *refs: norm_back_kernel(layer, len(parts), *refs),
        in_specs=[vmem] * (3 + len(parts)) + [ANY_SPEC] * len(earlier),
        out_shape=[
            jax.ShapeDtypeStruct((HALF, D), F32),
            jax.ShapeDtypeStruct((HALF, D), BF),
            jax.ShapeDtypeStruct((8, D), F32),
        ],
        compiler_params=pltpu.CompilerParams(vmem_limit_bytes=VMEM_LIMIT),
        cost_estimate=SMALL_COST,
        name="norm_back",
    )(grad_next, hidden, *parts, model_vec, *earlier)


def fold_kernel(count, z_ref, own_ref, other_ref, *refs):
    outs = refs[len(refs) - count :]
    totals = [own_ref[k].astype(F32) + other_ref[k].astype(F32) for k in range(ZS)]
    for k in range(ZS):
        outs[k][...] = totals[k].astype(outs[k].dtype)
    if len(outs) > ZS:
        outs[ZS][...] = jnp.where(z_ref[0] == 0, totals[1], totals[3]).astype(BF)


def fold(z_array, own, other, kinds, earlier=()):
    return pl.pallas_call(
        lambda *refs: fold_kernel(len(kinds), *refs),
        in_specs=[pl.BlockSpec(memory_space=pltpu.SMEM)]
        + [pl.BlockSpec(memory_space=pltpu.VMEM)] * 2
        + [ANY_SPEC] * len(earlier),
        out_shape=[jax.ShapeDtypeStruct((HALF, D), kind) for kind in kinds],
        compiler_params=pltpu.CompilerParams(vmem_limit_bytes=VMEM_LIMIT),
        cost_estimate=SMALL_COST,
        name="fold",
    )(z_array, own, other, *earlier)


class Place:
    def __init__(self, ny):
        self.ny = ny
        self.z = lax.axis_index("z")
        self.y = lax.axis_index("y")
        self.x = lax.axis_index("x")
        self.c = lax.axis_index("c")

    def own_first(self, lower, upper, index, axis):
        mine = jnp.where(index == 0, lower, upper)
        other = jnp.where(index == 0, upper, lower)
        return jnp.concatenate([mine, other], axis)

    def to_local(self, array):
        parts = array.reshape(*array.shape[:-1], ZS, self.ny, -1)
        parts = jnp.swapaxes(parts, -2, -3).reshape(*array.shape[:-1], 2, -1)
        lower, upper = parts[..., 0, :], parts[..., 1, :]
        if self.ny == 2:
            return self.own_first(lower, upper, self.y, -1)
        return jnp.concatenate([lower, upper], -1)

    def from_local(self, array):
        half = array.shape[-1] // 2
        lower, upper = array[..., :half], array[..., half:]
        if self.ny == 2:
            array = self.own_first(lower, upper, self.y, -1)
        parts = array.reshape(*array.shape[:-1], self.ny, ZS, -1)
        return jnp.swapaxes(parts, -2, -3).reshape(*array.shape)

    def y_columns(self, array):
        if self.ny == 2:
            return jnp.concatenate([array, swap(array, "y")], -1)
        return lax.all_gather(array, "y", axis=array.ndim - 1, tiled=True)

    def y_place(self, array):
        if self.ny == 2:
            other = swap(array, "y")
            return self.own_first(array, other, self.y, -1)
        return lax.all_gather(array, "y", axis=array.ndim - 1, tiled=True)


def after(array, *earlier):
    return lax.optimization_barrier((array, *earlier))[0]


def gather_z(array):
    return [array] + [shift_z(array, k) for k in range(1, ZS)]


def line_z(array, pairs):
    return lax.ppermute(array, "z", pairs)


def gather_rows(rows, *earlier):
    mine = gather_z(rows)
    return mine + [swap(after(part, *earlier) if earlier else part, "c") for part in mine]


def gather_line(place, rows, *deadlines, second=()):
    far = swap(rows, "c")
    up_one = line_z(rows, [(0, 1), (1, 2), (2, 3)])
    down_one = line_z(rows, [(3, 2), (2, 1), (1, 0)])
    up_one, down_one = after(up_one, far, *second), after(down_one, *second)
    up_two = line_z(up_one, [(1, 2), (2, 3)])
    down_two = line_z(down_one, [(2, 1), (1, 0)])
    two = up_two + down_two
    if deadlines:
        two = after(two, *deadlines)
    far_two = swap(two, "c")
    end = after(line_z(two, [(2, 3), (1, 0)]), far_two)
    one = jnp.where(place.z == 0, end, up_one)
    three = jnp.where(place.z == ZS - 1, end, down_one)
    return [rows, one, two, three, far, swap(one, "c"), far_two, swap(three, "c")]


def scatter_rows(z_array, parts, *earlier):
    own, other = parts
    if earlier:
        other = after(other, *earlier)
    terms = fold(z_array, own, swap(other, "c"), (F32, BF, BF, BF))
    return [terms[0]] + [shift_z(terms[k], -k) for k in range(1, ZS)]


def scatter_line(z_array, parts, first=(), then=(), mid=(), last=(), tokens=()):
    own, other = parts
    if first:
        other = after(other, *first)
    other = swap(other, "c")
    if then:
        other = after(other, *then)
    own, one, two, three, end = fold(z_array, own, other, (F32, F32, F32, F32, BF), tokens)
    end = line_z(end, [(0, 1), (3, 2)])
    two = (two + end.astype(F32)).astype(BF)
    if mid:
        two = after(two, *mid)
    down_two = line_z(two, [(2, 1), (3, 2)])
    up_two = line_z(two, [(1, 2), (0, 1)])
    one = (one + down_two.astype(F32)).astype(BF)
    three = (three + up_two.astype(F32)).astype(BF)
    if last:
        one, three = after(one, *last), after(three, *last)
    down_one = line_z(one, [(1, 0), (2, 1), (3, 2)])
    up_one = line_z(three, [(0, 1), (1, 2), (2, 3)])
    return [own, down_one, up_one]


def whole_spec(shape):
    return pl.BlockSpec(shape, lambda *_: (0,) * len(shape))


def quarter(z_ref, k, sign):
    return (z_ref[0] + sign * k + ZS) % ZS


def weight_specs(kind, layer, dd, heads_n, ffn_n, sign):
    fronts = [
        pl.BlockSpec((1, 3, dd, heads_n), lambda k, z: (layer, 0, 0, quarter(z, k, sign))),
        pl.BlockSpec((1, dd, ffn_n), lambda k, z: (layer, 0, quarter(z, k, sign))),
    ]
    backs = [
        pl.BlockSpec((1, heads_n, dd), lambda k, z: (layer, quarter(z, k, sign), 0)),
        pl.BlockSpec((1, ffn_n, dd), lambda k, z: (layer, quarter(z, k, sign), 0)),
    ]
    return {"front": fronts, "back": backs, "both": fronts + backs}[kind]


def pack_kernel(kind, z_ref, *refs):
    refs, outs = refs[:-ZS], refs[-ZS:]
    parts = []
    if kind != "back":
        parts += [refs[0][0, which].T for which in range(3)] + [refs[1][0].T]
    if kind != "front":
        parts += [refs[-2][0], refs[-1][0]]
    block = jnp.concatenate(parts, 0).astype(BF)
    for k in range(ZS):

        @pl.when(pl.program_id(0) == k)
        def _():
            outs[k][...] = block


def pack(kind, layer, z_array, arrays, dd, heads_n, ffn_n):
    n = {"front": 3 * heads_n + ffn_n, "back": heads_n + ffn_n, "both": 4 * heads_n + 2 * ffn_n}[kind]
    return pl.pallas_call(
        lambda *refs: pack_kernel(kind, *refs),
        grid_spec=pltpu.PrefetchScalarGridSpec(
            num_scalar_prefetch=1,
            grid=(ZS,),
            in_specs=weight_specs(kind, layer, dd, heads_n, ffn_n, 1),
            out_specs=[whole_spec((n, dd))] * ZS,
        ),
        out_shape=[jax.ShapeDtypeStruct((n, dd), BF)] * ZS,
        compiler_params=pltpu.CompilerParams(vmem_limit_bytes=VMEM_LIMIT),
        cost_estimate=pl.CostEstimate(
            flops=0, bytes_accessed=6 * ZS * n * dd, transcendentals=0
        ),
        name="pack_" + kind,
    )(z_array, *arrays)


def stack_kernel(*refs):
    dd = refs[0].shape[1]
    for at, ref in enumerate(refs[:-1]):
        refs[-1][:, at * dd : (at + 1) * dd] = ref[...]


def stack(pieces):
    n, dd = pieces[0].shape
    if dd % 128:
        return jnp.concatenate(pieces, 1)
    return pl.pallas_call(
        stack_kernel,
        out_shape=jax.ShapeDtypeStruct((n, len(pieces) * dd), BF),
        compiler_params=pltpu.CompilerParams(vmem_limit_bytes=VMEM_LIMIT),
        cost_estimate=SMALL_COST,
        name="stack",
    )(*pieces)


def stack_rows_kernel(*refs):
    for at, ref in enumerate(refs[:-1]):
        refs[-1][at * HALF : (at + 1) * HALF] = ref[...]


def stack_rows(rows):
    return pl.pallas_call(
        stack_rows_kernel,
        out_shape=jax.ShapeDtypeStruct((len(rows) * HALF, D), BF),
        compiler_params=pltpu.CompilerParams(vmem_limit_bytes=VMEM_LIMIT),
        cost_estimate=SMALL_COST,
        name="stack_rows",
    )(*rows)


def spread_xy(kind, near, *earlier):
    cut = cut_of(kind)
    on_x, on_y = swap(near, "x"), swap(near, "y")
    one, two = on_x[:cut], on_y[cut:]
    if earlier:
        one, two = after(one, *earlier), after(two, *earlier)
    return near, on_y, on_x, swap(one, "y"), swap(two, "x")


def weight_grads(kind, left, right, cut):
    n, half = left.shape[1] // 2, right.shape[1] // 2
    cut = min(cut, n)
    lower, upper = right[:, :half], right[:, half:]
    own, other = left[:, :n], left[:, n:]
    return [
        dot_tn(one, two).astype(BF) if one.shape[1] else jnp.zeros((0, half), BF)
        for one, two in (
            (other[:, :cut], upper),
            (other[:, cut:], upper),
            (own, upper),
            (other, lower),
            (own, lower),
        )
    ]


def bump_kernel(count, *refs):
    parts, (one_ref, two_ref), (y_ref, x_ref) = refs[: 2 * count], refs[2 * count :][:2], refs[-2:]
    at = 0
    for on_y, on_x in zip(parts[:count], parts[count:]):
        rows = slice(at, at + on_y.shape[0])
        y_ref[rows] = on_y[...]
        x_ref[rows] = on_x[...]
        at += on_y.shape[0]
    cut = one_ref.shape[0]
    y_ref[:cut] = add_low(y_ref[:cut], one_ref[...])
    x_ref[cut:] = add_low(x_ref[cut:], two_ref[...])


def bump(on_y, on_x, far_one, far_two, earlier=()):
    n = sum(part.shape[0] for part in on_y)
    vmem = pl.BlockSpec(memory_space=pltpu.VMEM)
    return pl.pallas_call(
        lambda *refs: bump_kernel(len(on_y), *refs),
        in_specs=[vmem] * (2 * len(on_y) + 2) + [ANY_SPEC] * len(earlier),
        out_shape=[jax.ShapeDtypeStruct((n, on_y[0].shape[1]), BF)] * 2,
        compiler_params=pltpu.CompilerParams(vmem_limit_bytes=VMEM_LIMIT),
        cost_estimate=SMALL_COST,
        name="bump",
    )(*on_y, *on_x, far_one, far_two, *earlier)


def split_kernel(count, z_ref, *refs):
    near, (y_ref, x_ref, *_), outs = refs[:count], refs[count:], refs[-ZS:]
    value = jnp.concatenate([part[...] for part in near], 0).astype(F32)
    value = (value + y_ref[...].astype(F32) + x_ref[...].astype(F32)).astype(BF)
    for k in range(ZS):

        @pl.when(pl.program_id(0) == k)
        def _():
            outs[k][...] = value


def split(z_array, near, from_y, from_x, earlier=()):
    n, width = from_y.shape
    dd = width // ZS
    return pl.pallas_call(
        lambda *refs: split_kernel(len(near), *refs),
        grid_spec=pltpu.PrefetchScalarGridSpec(
            num_scalar_prefetch=1,
            grid=(ZS,),
            in_specs=[
                pl.BlockSpec((part.shape[0], dd), lambda k, z: (0, quarter(z, k, 1)))
                for part in (*near, from_y, from_x)
            ]
            + [ANY_SPEC] * len(earlier),
            out_specs=[whole_spec((n, dd))] * ZS,
        ),
        out_shape=[jax.ShapeDtypeStruct((n, dd), BF)] * ZS,
        compiler_params=pltpu.CompilerParams(vmem_limit_bytes=VMEM_LIMIT),
        cost_estimate=SMALL_COST,
        name="split",
    )(z_array, *near, from_y, from_x, *earlier)


def add_low(left, right):
    return (left.astype(F32) + right.astype(F32)).astype(BF)


def sum_plain(place, grads):
    own = jnp.concatenate([jnp.concatenate([g[4], g[2]], 1) for g in grads], 0)
    other = [jnp.concatenate([g[3], jnp.concatenate([g[0], g[1]], 0)], 1) for g in grads]
    both = add_low(own, swap(jnp.concatenate(other, 0), "x"))
    total = lax.psum_scatter(both, "y", scatter_dimension=1, tiled=True)
    n, width = total.shape
    dd = width // ZS
    return [lax.dynamic_slice(total, (0, (place.z + k) % ZS * dd), (n, dd)) for k in range(ZS)]


def adam_kernel(kind, heads_n, ffn_n, offset, rates, z_ref, *refs):
    pieces, states, outs = refs[:ZS], refs[ZS : ZS + 6], refs[-9:-1]
    refs[-1][...] = jnp.zeros_like(refs[-1])
    for k in range(ZS):

        @pl.when(pl.program_id(0) == k)
        def _():
            split = (3 if kind == "front" else 1) * heads_n
            piece = pieces[k][offset : offset + split + ffn_n]
            if kind == "front":
                grads = [
                    jnp.stack(
                        [
                            piece[which * heads_n : (which + 1) * heads_n].astype(F32).T
                            for which in range(3)
                        ]
                    )[None],
                    piece[split:].astype(F32).T[None],
                ]
            else:
                grads = [piece[:split].astype(F32)[None], piece[split:].astype(F32)[None]]
            for at, grad in enumerate(grads):
                weight, first, second = [ref[...] for ref in states[at * 3 : at * 3 + 3]]
                outs[at * 4][...] = grad
                new = adamw(weight, grad, first, second, rates[at], DECAY)
                for ref, value in zip(outs[at * 4 + 1 : at * 4 + 4], new):
                    ref[...] = value


def adam(kind, layer, z_array, pieces, offset, states, rates, earlier, tokens, heads_n, ffn_n):
    n, dd = pieces[0].shape
    first, second = weight_specs(kind, layer, dd, heads_n, ffn_n, -1)
    shapes = [jax.ShapeDtypeStruct(states[at].shape, F32) for at in (0, 3) for _ in range(4)]
    earlier = list(earlier or [])
    return pl.pallas_call(
        lambda *refs: adam_kernel(kind, heads_n, ffn_n, offset, rates, *refs),
        grid_spec=pltpu.PrefetchScalarGridSpec(
            num_scalar_prefetch=1,
            grid=(ZS,),
            in_specs=[whole_spec((n, dd))] * ZS
            + [first] * 3
            + [second] * 3
            + [ANY_SPEC] * (len(earlier) + len(tokens)),
            out_specs=[first] * 4 + [second] * 4 + [whole_spec((8, 128))],
        ),
        out_shape=shapes + [jax.ShapeDtypeStruct((8, 128), F32)],
        input_output_aliases={1 + ZS + 6 + at: at for at in range(len(earlier))},
        compiler_params=pltpu.CompilerParams(vmem_limit_bytes=VMEM_LIMIT),
        cost_estimate=SMALL_COST,
        name="adam_" + kind,
    )(z_array, *pieces, *states, *earlier, *tokens)


def tables(positions):
    half = ROT // 2
    places = jnp.maximum(positions, 0).astype(F32)
    frequency = 10000.0 ** (-(2.0 / ROT) * jnp.arange(half).astype(F32))
    angles = places[..., None] * frequency
    both = jnp.concatenate([jnp.cos(angles), jnp.sin(angles)], -1)
    pick = np.zeros((ROT, 3, 2, HEAD_DIM), np.float32)
    for at in range(half):
        pick[at, 0, :, at] = pick[at, 0, :, half + at] = 1.0
        pick[half + at, 1, :, at] = -1.0
        pick[half + at, 2, :, half + at] = 1.0
    rest = np.zeros((3, 2, HEAD_DIM), np.float32)
    rest[0, :, ROT:] = 1.0
    table = jnp.dot(both, pick.reshape(ROT, -1), precision=lax.Precision.HIGHEST)
    return table + rest.reshape(-1)


def adamw(weight, grad, first, second, rate, decay):
    first_new = BETA_ONE * first + (1.0 - BETA_ONE) * grad
    second_new = BETA_TWO * second + (1.0 - BETA_TWO) * grad * grad
    first_hat = first_new / (1.0 - BETA_ONE**STEP)
    second_hat = second_new / (1.0 - BETA_TWO**STEP)
    weight_new = weight - rate * (first_hat / (jnp.sqrt(second_hat) + ADAM_EPS) + decay * weight)
    return (first_new, second_new, weight_new)


def source_lane(at, y):
    return (at % ZS) * 2 + (at // ZS + y) % 2


def take_kernel(place_ref, rows_ref, grads_ref, live_ref, start_ref, low_ref):
    dd = D // (2 * ZS)
    for at in range(2 * ZS):
        lanes = pl.ds(pl.multiple_of(source_lane(at, place_ref[1]) * dd, 128), dd)
        to = slice(at * dd, (at + 1) * dd)
        start_ref[:, to] = rows_ref[:, lanes]
        low_ref[:, to] = (grads_ref[:, lanes].astype(F32) * live_ref[...]).astype(BF)


def take(place, activations, cotangent, live):
    m = place.x * 2 + place.c
    if place.ny != 2:
        mine = [
            place.to_local(lax.dynamic_slice_in_dim(array, m * HALF, HALF, 0))
            for array in (activations, cotangent)
        ]
        return mine[0], (mine[1].astype(F32) * live).astype(BF)
    where = jnp.stack([m, place.y]).astype(jnp.int32)
    return pl.pallas_call(
        take_kernel,
        grid_spec=pltpu.PrefetchScalarGridSpec(
            num_scalar_prefetch=1,
            grid=(1,),
            in_specs=[pl.BlockSpec((HALF, D), lambda at, ref: (ref[0], 0))] * 2
            + [pl.BlockSpec((HALF, 1), lambda at, ref: (0, 0))],
            out_specs=[pl.BlockSpec((HALF, D), lambda at, ref: (0, 0))] * 2,
        ),
        out_shape=[jax.ShapeDtypeStruct((HALF, D), BF)] * 2,
        cost_estimate=pl.CostEstimate(flops=0, bytes_accessed=8 * HALF * D, transcendentals=0),
        name="take",
    )(where, activations, cotangent, live)


def give_kernel(place_ref, *refs):
    dd = D // (2 * ZS)
    for block in range(4):

        @pl.when(pl.program_id(0) == block)
        def _():
            for at in range(2 * ZS):
                lanes = pl.ds(pl.multiple_of(source_lane(at, place_ref[2]) * dd, 128), dd)
                refs[-1][:, lanes] = refs[block][:, at * dd : (at + 1) * dd].astype(F32)


def give(place, blocks):
    where = jnp.stack([place.x, place.c, place.y]).astype(jnp.int32)
    if place.ny != 2:
        result = jnp.zeros((4 * HALF, D), F32)
        for at, block in enumerate(blocks):
            row = ((place.x + at // 2) % 2) * 2 + (place.c + at % 2) % 2
            result = lax.dynamic_update_slice(
                result, place.from_local(block).astype(F32), (row * HALF, 0)
            )
        return result

    def target(at, ref):
        return (((ref[0] + at // 2) % 2) * 2 + (ref[1] + at % 2) % 2, 0)

    return pl.pallas_call(
        give_kernel,
        grid_spec=pltpu.PrefetchScalarGridSpec(
            num_scalar_prefetch=1,
            grid=(4,),
            in_specs=[whole_spec((HALF, D))] * 4,
            out_specs=pl.BlockSpec((HALF, D), target),
        ),
        out_shape=jax.ShapeDtypeStruct((4 * HALF, D), F32),
        compiler_params=pltpu.CompilerParams(vmem_limit_bytes=VMEM_LIMIT),
        cost_estimate=SMALL_COST,
        name="give",
    )(where, *blocks)


def per_device(
    ny,
    activations,
    cotangent,
    positions,
    w_qkv,
    w_out,
    w_up,
    w_down,
    vec_model,
    vec_head,
    vec_ffn,
    first_qkv,
    first_out,
    first_up,
    first_down,
    first_model,
    first_head,
    first_ffn,
    second_qkv,
    second_out,
    second_up,
    second_down,
    second_model,
    second_head,
    second_ffn,
):
    place = Place(ny)
    dd = w_up.shape[1]
    heads_n = w_qkv.shape[3] // ZS
    ffn_n = w_up.shape[2] // ZS
    sizes = (dd, heads_n, ffn_n)
    z_array = place.z.reshape(1).astype(jnp.int32)

    model_own = vec_model.astype(BF).reshape(LAYERS * 4, dd)
    head_own, ffn_own = vec_head.astype(BF), vec_ffn.astype(BF)
    if ny == 2:
        first = jnp.concatenate(
            [model_own.reshape(-1), head_own.reshape(-1), ffn_own.reshape(-1)]
        )
        far = swap(first, "y")
        ends = [model_own.size, model_own.size + head_own.size, first.size]
        model_far, head_far, ffn_far = [
            far[start:end].reshape(own.shape)
            for start, end, own in zip([0] + ends, ends, (model_own, head_own, ffn_own))
        ]
        model_y = jnp.stack([model_own, model_far], 1)
        head_y = place.own_first(head_own, head_far, place.y, -1)
        ffn_y = place.own_first(ffn_own, ffn_far, place.y, -1)
    else:
        model_y = lax.all_gather(model_own, "y", axis=1)
        head_y = lax.all_gather(head_own, "y", axis=2, tiled=True)
        ffn_y = lax.all_gather(ffn_own, "y", axis=1, tiled=True)
    slim = jnp.concatenate([head_y.reshape(LAYERS, -1), ffn_y], 1)
    places_x = lax.dynamic_slice_in_dim(positions, place.x * ROWS, ROWS)
    places_x = place.own_first(places_x[:HALF], places_x[HALF:], place.c, 0)
    if ny == 2:
        pieces_front = pack("front", 0, z_array, (w_qkv, w_up), *sizes)
        slim = after(slim, *pieces_front)
    mine = jnp.concatenate([model_y.reshape(-1), places_x.astype(BF)])
    slim_x = swap(slim, "x")
    bias = jnp.concatenate([slim, slim_x], 1).astype(F32)
    packed = jnp.stack(
        [mine] + [lax.ppermute(mine, "z", [(i, i ^ k) for i in range(ZS)]) for k in range(1, ZS)]
    )
    if ny == 2:
        pieces_front = [after(piece, packed, slim_x) for piece in pieces_front]
        came_front = [pieces_front[0]] + [shift_z(pieces_front[k], k) for k in range(1, ZS)]
        on_x, on_y = swap(pieces_front[0], "x"), swap(pieces_front[0], "y")
        later_z = after(z_array, on_x, on_y)
        pieces_next = pack("both", 1, later_z, (w_qkv, w_up, w_out, w_down), *sizes)
        pieces_back = pack("back", 0, later_z, (w_out, w_down), *sizes)
        cut = cut_of("front")
        ready = *pieces_next, *pieces_back
        far_one, far_two = after(on_x[:cut], *ready), after(on_y[cut:], *ready)
        own_front = pieces_front[0], on_y, on_x, swap(far_one, "y"), swap(far_two, "x")
    everyone = jnp.arange(ZS, dtype=jnp.int32)
    by_z = jnp.take(packed, everyone ^ place.z, axis=0)
    model_vec = by_z[:, : LAYERS * 4 * ny * dd].reshape(ZS, LAYERS * 4, ny, dd)
    model_vec = model_vec.transpose(1, 2, 0, 3).reshape(LAYERS * 4, D)
    places = jnp.take(by_z[:, LAYERS * 4 * ny * dd :], (place.z - everyone) % ZS, axis=0)
    places = places.astype(F32).astype(jnp.int32)

    order = (jnp.arange(ROWS, dtype=jnp.int32) + place.c * HALF) % ROWS
    starts = order - jnp.maximum(places, 0)
    seen = (order[None, None, :] <= order[None, :, None]) & (
        order[None, None, :] >= starts[:, :, None]
    )
    mask = jnp.where(seen, 0.0, MASKED).astype(F32)
    table = tables(jnp.swapaxes(places.reshape(ZS, 2, HALF), 0, 1))

    mine = place.x * ROWS + place.c * HALF
    live = (lax.dynamic_slice_in_dim(positions, mine, HALF) >= 0).astype(F32)[:, None]
    if ny == 2:
        live = after(live, *own_front[1:3])
    start, last_low = take(place, activations, cotangent, live)

    kernel_z = z_array if ny == 2 else jnp.zeros_like(z_array)
    n_front, n_back = 3 * heads_n + ffn_n, heads_n + ffn_n
    n_both = n_front + n_back
    arrays = {"front": (w_qkv, w_up), "back": (w_out, w_down), "both": (w_qkv, w_up, w_out, w_down)}

    def packed_pieces(kind, layer):
        return pack(kind, layer, z_array, arrays[kind], *sizes)

    def send_z(pieces, *earlier):
        if earlier:
            pieces = [pieces[0]] + [after(piece, *earlier) for piece in pieces[1:]]
        return [pieces[0]] + [shift_z(pieces[k], k) for k in range(1, ZS)]

    def spread_plain(kind, layer):
        pieces = send_z(packed_pieces(kind, layer))
        n = pieces[0].shape[0]
        joined = jnp.zeros((n, ZS * dd), BF)
        for k, piece in enumerate(pieces):
            joined = lax.dynamic_update_slice(joined, piece, (0, (place.z - k) % ZS * dd))
        own = place.y_columns(joined).reshape(n, 2, ZS, -1)
        own = jnp.stack([own[:, :, -k % ZS] for k in ORDER], 2).reshape(n, D)
        other = swap(own, "x")
        cut, half = cut_of(kind), D // 2
        return own[:, :half], own[:, half:], other[:, :half], other[:cut, half:], other[cut:, half:]

    def layout_of(kind, chunks, first=0):
        n, cut = {"front": n_front, "back": n_back}[kind], cut_of(kind)
        ids = [tuple(5 * c + at for c in range(chunks)) for at in range(5)]
        far = [(ids[3], 0, cut), (ids[4], 0, n - cut)]
        return (*((ids[at], 0, n) for at in range(3)), far)

    both_cut = cut_of("both")
    chunks = 3 if ny == 2 else 1
    ids = [tuple(5 * c + at for c in range(chunks)) for at in range(5)]
    merged = (
        (*((ids[at], 0, n_front) for at in range(3)), [(ids[3], 0, both_cut), (ids[4], 0, n_front - both_cut)]),
        (*((ids[at], n_front, n_both) for at in range(3)), [(ids[4], n_front - both_cut, n_both - both_cut)]),
    )

    hidden, normed = norm(0, False, start, (), model_vec)
    if ny == 2:
        came_front[1] = after(came_front[1], start)
        came_back = send_z(pieces_back, *came_front[1:])
        rest_front = list(
            spread_xy("front", stack([after(came_front[1], *own_front[3:]), *came_front[:1:-1]]))
        )
        fronts = [*own_front, *rest_front]
        rest_front[1] = after(rest_front[1], table, mask)
        near_back = stack([came_back[0], after(came_back[1], *rest_front[3:]), *came_back[:1:-1]])
        on_x, on_y = swap(near_back, "x"), swap(near_back, "y")
        rows = gather_line(
            place, after(normed, *came_back[1:]), near_back, second=rest_front[1:3]
        )
        came_next = send_z(pieces_next, *rows[1:4])
    else:
        rows = gather_line(place, normed)
        fronts = spread_plain("front", 0)
        backs = spread_plain("back", 0)
    layouts = layout_of("front", 2 if ny == 2 else 1), layout_of("back", 1)
    shift = len(fronts)
    move = lambda part: (tuple(at + shift for at in part[0]), *part[1:])
    joint = layouts[0], (*map(move, layouts[1][:3]), [move(part) for part in layouts[1][3]])

    normed, qkv, logs, left, slope = front(
        kernel_z, rows, layouts[:1], fronts, bias[0:1], table, mask
    )
    kept = [(hidden, normed, qkv, logs, left, slope)]
    if ny == 2:
        cut, ready = cut_of("back"), (left, came_next[1], came_next[3])
        far_one, far_two = after(on_x[:cut], *ready), after(on_y[cut:], *ready)
        backs = near_back, on_y, on_x, swap(far_one, "y"), swap(far_two, "x")
        first_next = spread_xy("both", after(came_next[0], *backs[3:]))
        mid_next = stack([came_next[1], came_next[3]])
        left = after(left, mid_next)
    own, other = back(kernel_z, left, layouts[1], backs)
    if ny == 2:
        last_piece = after(came_next[2], other)
        mid_next = spread_xy("both", after(mid_next, *first_next[1:3]))
        last_next = spread_xy("both", after(last_piece, *mid_next[1:3]))
        spread = [*first_next, *mid_next, *last_next]
        parts = scatter_line(z_array, (own, other), first=(last_piece, *first_next[1:3]))
        parts[2] = after(parts[2], *mid_next[1:3], *first_next[3:])
    else:
        spread = spread_plain("both", 1)
        parts = scatter_line(z_array, (own, other))
    hidden, normed = norm(1, False, hidden, parts, model_vec)
    if ny == 2:
        rows = gather_line(place, normed, second=(*last_next[1:3], *mid_next[3:]))
    else:
        rows = gather_line(place, normed)
    mine_z = rows[1:4]
    normed, qkv, logs, left, slope, own, other = front(
        kernel_z, rows, merged, spread, bias[1:2], table, mask
    )
    kept.append((hidden, normed, qkv, logs, left, slope))
    rows = gather_rows(after(last_low, *mine_z))
    rest = scatter_rows(z_array, (own, other), *rows[1:4])
    rows[4] = after(rows[4], rest[0])

    outs = {"front": None, "back": None}
    states = {
        "front": (w_qkv, first_qkv, second_qkv, w_up, first_up, second_up),
        "back": (w_out, first_out, second_out, w_down, first_down, second_down),
    }
    rate_in = 3.0 / math.sqrt(D)
    rates = {
        "front": (rate_in, rate_in),
        "back": (12.0 / math.sqrt(D), 3.0 / math.sqrt(FF)),
    }

    def flat(array):
        return array.reshape(ALL_ROWS, -1)

    def first_hop(grads, earlier=()):
        far_one = jnp.concatenate([g[0] for g in grads], 0) if len(grads) > 1 else grads[0][0]
        far_two = jnp.concatenate([g[1] for g in grads], 0) if len(grads) > 1 else grads[0][1]
        return bump(
            [g[2] for g in grads],
            [g[3] for g in grads],
            swap(far_one, "x"),
            swap(far_two, "y"),
            earlier,
        )

    def second_hop(on_y, on_x):
        return swap(on_y, "y"), swap(on_x, "x")

    def step(kind, layer, pieces, offset, tokens=()):
        *outs[kind], token = adam(
            kind, layer, z_array, pieces, offset, states[kind], rates[kind], outs[kind], tokens, heads_n, ffn_n
        )
        return token

    sums, slims = {}, {}
    hidden_in, normed, qkv, logs, left, slope = kept[1]
    left_grad, own, other, slims[1] = reverse(
        kernel_z, rows, merged, spread, slope, qkv, logs, table, mask
    )
    grads = [
        weight_grads("back", flat(left), stack_rows(rows), cut_of("back")),
        weight_grads("front", flat(left_grad), flat(normed), cut_of("front")),
    ]
    (result,) = norm(LAYERS, True, hidden, rest, model_vec)
    result_x = swap(result, "x")
    results = [result, swap(result, "c"), result_x, swap(result_x, "c")]
    if ny == 2:
        hops = [first_hop(grads[:1])]
        seconds = [second_hop(*hops[0])]
        parts = scatter_line(z_array, (own, other), rest[1:], last=(*hops[0], result_x))
        late_far = [after(part, *seconds[0], *parts[1:]) for part in grads[1][:2]]
        hops.append(first_hop([late_far + grads[1][2:]]))
        grad_next, low, sums[1] = norm_back(1, last_low, hidden_in, parts, model_vec)
        seconds.append(second_hop(*hops[1]))
        rows = gather_line(place, low, *hops[1], second=(results[1], results[3]))
        came_one = [send_z(split(z_array, grads[0][4:], *seconds[0]), *rows[5:]), None]
    else:
        parts = scatter_line(z_array, (own, other))
        grad_next, low, sums[1] = norm_back(1, last_low, hidden_in, parts, model_vec)
        rows = gather_line(place, low)
        came_one = [send_z(sum_plain(place, grads[:1])), sum_plain(place, grads[1:])]
    hidden_in, normed, qkv, logs, left, slope = kept[0]
    left_grad, own, other, slims[0] = reverse(
        kernel_z, rows, joint, [*fronts, *backs], slope, qkv, logs, table, mask
    )
    left_grad = after(left_grad, *came_one[0][1:])
    if ny == 2:
        came_one[1] = split(z_array, grads[1][4:], *seconds[1], [slims[0]])
    grads_front = weight_grads("front", flat(left_grad), flat(normed), cut_of("front"))
    came_one[1] = send_z(came_one[1], *came_one[0][1:])
    if ny == 2:
        hop_front = first_hop([grads_front])
        second_front = second_hop(*hop_front)
        rows = [after(row, hop_front[0]) for row in rows]
    grads_back = weight_grads("back", flat(left), stack_rows(rows), cut_of("back"))
    tokens = [step("back", 1, came_one[0], 0), step("front", 1, came_one[1], 0)]
    result_rows = give(place, results)
    if ny == 2:
        parts = scatter_line(
            z_array,
            (own, other),
            (came_one[1][1], came_one[1][3], *hop_front),
            came_one[1][2:3],
            second_front,
        )
        near_front = after(grads_front[4], *grads_back[:2])
        sum_front = split(z_array, [near_front], *second_front)
        came_front = send_z(sum_front)
        late_far = [after(part, *second_front) for part in grads_back[:2]]
        hop_back = first_hop([late_far + grads_back[2:]])
        second_back = second_hop(*(after(p, came_front[1], came_front[3]) for p in hop_back))
        sum_back = split(z_array, grads_back[4:], *second_back)
        came_back = send_z(sum_back)
        norm_parts = [*parts[:2], after(parts[2], *came_front[1:], *second_back)]
    else:
        parts = scatter_line(z_array, (own, other))
        came_front = send_z(sum_plain(place, [grads_front]))
        sum_back = sum_plain(place, [grads_back])
        came_back = send_z(sum_back)
        norm_parts = parts
    grad_next, low, sums[0] = norm_back(
        0, grad_next, hidden_in, norm_parts, model_vec, [*tokens, result_rows]
    )
    came_front = [came_front[0], *(after(piece, sum_back[0]) for piece in came_front[1:])]
    token = step("front", 0, came_front, 0)
    step("back", 0, came_back, 0, [token])
    late = sum_back[0]

    low_x = swap(low, "x")
    low, low_x = [after(part, *came_back[1:]) for part in (low, low_x)]
    both = after(jnp.concatenate([slims[0], slims[1]], 0), late)
    n = both.shape[1] // 2
    slim = both[:, :n] + swap(both[:, n:], "x")
    heads = slim[:, : 3 * heads_n].reshape(LAYERS, 3, ny, -1)
    ffns = slim[:, 3 * heads_n :].reshape(LAYERS, ny, -1)
    slim = jnp.concatenate([heads.swapaxes(1, 2).reshape(LAYERS, ny, -1), ffns], 2)
    if ny == 2:
        mine, far = [jnp.where(place.y == at, slim[:, 0], slim[:, 1]) for at in range(2)]
        slim = mine + swap(far, "y")
    else:
        slim = lax.psum_scatter(slim, "y", scatter_dimension=1, tiled=False)
    at = 3 * heads_n // ny
    grad_head = slim[:, :at].reshape(LAYERS, 3, -1)
    grad_ffn = slim[:, at:]

    total = jnp.stack([sums[layer][:3] for layer in range(LAYERS)])
    total = total + swap(total, "x")
    total = total + swap(total, "c")
    if ny == 2:
        half = D // 2
        total = total[..., :half] + swap(total[..., half:], "y")
    else:
        total = lax.psum_scatter(total, "y", scatter_dimension=2, tiled=True)
    grad_model = lax.dynamic_slice_in_dim(total, place.z * dd, dd, 2)
    for k in range(1, ZS):
        grad_model = grad_model + shift_z(
            lax.dynamic_slice_in_dim(total, (place.z + k) % ZS * dd, dd, 2), k
        )
    grad_model = jnp.concatenate([grad_model, grad_model[:, 2:]], 1)

    small = []
    for weight, grad, first, second in (
        (vec_model, grad_model, first_model, second_model),
        (vec_head, grad_head, first_head, second_head),
        (vec_ffn, grad_ffn, first_ffn, second_ffn),
    ):
        small.append(grad)
        small.extend(adamw(weight, grad, first, second, 0.6, 0.0))
    ones, twos = outs["front"], outs["back"]
    return (
        result_rows,
        give(place, [low, swap(low, "c"), low_x, swap(low_x, "c")]),
        *ones[:4],
        *twos[:4],
        *ones[4:],
        *twos[4:],
        *small,
    )


def solution(mesh):
    n_dp, n_mp = mesh.devices.shape
    ny = n_dp // ZS
    split = Mesh(mesh.devices.reshape(ZS, ny, n_mp // 2, 2), ("z", "y", "x", "c"))
    dp, mp = ("z", "y"), ("x", "c")
    both = ("x", "c", "z", "y")
    params = (
        P(None, None, dp, mp),
        P(None, mp, dp),
        P(None, dp, mp),
        P(None, mp, dp),
        P(None, None, dp),
        P(None, None, both),
        P(None, both),
    )
    tokens = (P(dp, None), P(dp, None))
    return jax.shard_map(
        lambda *arrays: per_device(ny, *arrays),
        mesh=split,
        in_specs=(*tokens, P(dp), *params, *params, *params),
        out_specs=(*tokens, *(spec for spec in params for _ in range(4))),
        check_vma=False,
    )
```

```python
import math

import jax
import jax.numpy as jnp
import numpy as np
from jax import lax
from jax.experimental import pallas as pl
from jax.experimental.pallas import tpu as pltpu
from jax.sharding import Mesh
from jax.sharding import PartitionSpec as P

D = 2048
HEAD_DIM = 64
ROT = 32
FF = 8192
LAYERS = 2
STEP = 10
ROWS = 256
ZS = 4
HALF = 128
ORDER = (0, 1, 3, 2)
PAIR = 2 * HEAD_DIM

BETA_ONE = 0.9
BETA_TWO = 0.95
ADAM_EPS = 1e-08
DECAY = 0.1
NORM_EPS = 1e-05
MASKED = -1e30
BF = jnp.bfloat16
F32 = jnp.float32
VMEM_LIMIT = 58 * 2**20
SMALL_COST = pl.CostEstimate(flops=1024, bytes_accessed=1024, transcendentals=0)


def shift_z(array, step):
    return lax.ppermute(array, "z", [(i, (i + step) % ZS) for i in range(ZS)])


def swap(array, axis):
    return lax.ppermute(array, axis, [(0, 1), (1, 0)])


def dot_nt(left, right):
    return lax.dot_general(left, right, (((1,), (1,)), ((), ())), preferred_element_type=F32)


def dot_nn(left, right):
    return lax.dot_general(left, right, (((1,), (0,)), ((), ())), preferred_element_type=F32)


def dot_tn(left, right):
    return lax.dot_general(left, right, (((0,), (0,)), ((), ())), preferred_element_type=F32)


def turn(values, table):
    return (
        values * table[:, :PAIR]
        + pltpu.roll(values, PAIR - ROT // 2, 1) * table[:, PAIR : 2 * PAIR]
        + pltpu.roll(values, ROT // 2, 1) * table[:, 2 * PAIR :]
    )


def turn_back(grads, table):
    return (
        grads * table[:, :PAIR]
        - pltpu.roll(grads, PAIR - ROT // 2, 1) * table[:, PAIR : 2 * PAIR]
        - pltpu.roll(grads, ROT // 2, 1) * table[:, 2 * PAIR :]
    )


def low_lanes():
    return lax.broadcasted_iota(jnp.int32, (ROWS, PAIR), 1) < HEAD_DIM


def head_only(values, head):
    low_half = low_lanes()
    mine = low_half if head == 0 else jnp.logical_not(low_half)
    return jnp.where(mine, values, jnp.zeros_like(values))


def attend(queries, keys, values, mask):
    outs, logs = [], []
    for head in range(2):
        scores = dot_nt(head_only(queries, head), keys) + mask
        top = jnp.max(scores, -1, keepdims=True)
        exponent = jnp.exp(scores - top)
        total = jnp.sum(exponent, -1, keepdims=True)
        outs.append(dot_nn((exponent * (1.0 / total)).astype(BF), values))
        logs.append(jnp.broadcast_to(top + jnp.log(total), (ROWS, PAIR)))
    low_half = low_lanes()
    return jnp.where(low_half, *outs), jnp.where(low_half, *logs)


def attend_back(queries, keys, values, logs, grad, mask):
    grads = []
    for head in range(2):
        at = head * HEAD_DIM
        scores = dot_nt(head_only(queries, head), keys) + mask
        probs = jnp.exp(scores - logs[:, at : at + 1])
        grad_probs = dot_nt(head_only(grad, head), values)
        row_dot = jnp.sum(probs * grad_probs, -1, keepdims=True)
        grad_scores = (probs * (grad_probs - row_dot)).astype(BF)
        grads.append(
            (
                dot_nn(grad_scores, keys),
                dot_tn(grad_scores, queries),
                dot_tn(probs.astype(BF), grad),
            )
        )
    low_half = low_lanes()
    return [jnp.where(low_half, one, two) for one, two in zip(*grads)]


def cut_of(kind):
    return {"front": 3 * PAIR, "back": 2 * PAIR, "both": 6 * PAIR}[kind]


def nt_cols(left, segment):
    chunks, first, last = segment
    total, at = 0.0, 0
    for chunk in chunks:
        total = total + dot_nt(left[:, at : at + chunk.shape[1]], chunk[first:last])
        at += chunk.shape[1]
    return total


def nn_cols(left, segment):
    chunks, first, last = segment
    parts = [dot_nn(left, chunk[first:last]) for chunk in chunks]
    return parts[0] if len(parts) == 1 else jnp.concatenate(parts, 1)


def times_t(left, weights, x):
    near, on_y, on_x, far = weights
    half = left.shape[1] // 2
    lower, upper = left[:, :half], left[:, half:]
    if x == 0:
        return nt_cols(lower, near) + nt_cols(upper, on_y)
    parts = [nt_cols(upper, segment) for segment in far]
    return nt_cols(lower, on_x) + (parts[0] if len(parts) == 1 else jnp.concatenate(parts, 1))


def times(left, weights):
    near, on_y, on_x, far = weights
    n = near[2] - near[1]
    own, other = left[:, :n], left[:, n:]
    lower = nn_cols(own, near) + nn_cols(other, on_x)
    upper, at = nn_cols(own, on_y), 0
    for segment in far:
        rows = segment[2] - segment[1]
        upper = upper + nn_cols(other[:, at : at + rows], segment)
        at += rows
    return lower, upper


def bind(layout, refs):
    chunks = lambda part: (tuple(refs[at] for at in part[0]), part[1], part[2])
    near, on_y, on_x, far = layout
    return chunks(near), chunks(on_y), chunks(on_x), [chunks(part) for part in far]


def lanes_of(z_ref, k, y, dd):
    return pl.ds(pl.multiple_of(y * ZS * dd + (z_ref[0] - ORDER[k] + ZS) % ZS * dd, dd), dd)


def take_rows(z_ref, sources, relative, target=None):
    dd = relative.shape[1] // (2 * ZS)
    for slot in range(ZS):

        @pl.when(pl.program_id(0) == slot)
        def _():
            for core in range(2):
                source = sources[core * ZS + slot]
                rows = slice(core * HALF, (core + 1) * HALF)
                for y in range(2):
                    for k in range(ZS):
                        to = (y * ZS + k) * dd
                        relative[rows, to : to + dd] = source[:, lanes_of(z_ref, k, y, dd)]
                if target is not None:
                    target[core, 0] = source[...]


def put(ref, at, value):
    width = value.shape[1]
    ref[:, :, :, at : at + width] = value.astype(ref.dtype).reshape(2, 1, HALF, width)


def get(ref, at, width):
    return ref[:, :, :, at : at + width].reshape(ROWS, width)


def put_parts(z_ref, halves, own_ref, other_ref):
    for y, value in enumerate(halves):
        dd = value.shape[1] // ZS
        for k in range(ZS):
            lanes = lanes_of(z_ref, k, y, dd)
            part = value[:, k * dd : (k + 1) * dd].astype(BF)
            own_ref[0, :, lanes] = part[:HALF]
            other_ref[0, :, lanes] = part[HALF:]


def front_kernel(layouts, count, z_ref, *refs):
    rows, refs = refs[:8], refs[8:]
    weights, refs = refs[:count], refs[count:]
    fronts = bind(layouts[0], weights)
    bias_ref, table_ref, mask_ref, normed_ref, qkv_ref, log_ref, left_ref, slope_ref = refs[:8]
    relative = refs[-1]
    take_rows(z_ref, rows, relative, normed_ref)
    normed = relative[...]
    table = get(table_ref, 0, 3 * PAIR)
    n = fronts[0][2] - fronts[0][1]
    ffn_n = n - 3 * PAIR
    root = math.sqrt(2.0 / math.pi)
    for x in range(2):
        both = times_t(normed, fronts, x) + bias_ref[:, x * n : (x + 1) * n]
        gate = both[:, 3 * PAIR :]
        square = gate * gate
        bend = jnp.tanh(root * gate * (1.0 + 0.044715 * square))
        half_up = 0.5 + 0.5 * bend
        put(left_ref, x * (PAIR + ffn_n) + PAIR, gate * half_up)
        slope = half_up + (0.5 * gate) * (1.0 - bend * bend) * (
            root + (3.0 * 0.044715 * root) * square
        )
        put(slope_ref, x * ffn_n, slope)
        queries = turn(both[:, :PAIR], table).astype(BF) * jnp.asarray(HEAD_DIM**-0.5, BF)
        keys = turn(both[:, PAIR : 2 * PAIR], table).astype(BF)
        values = both[:, 2 * PAIR : 3 * PAIR].astype(BF)
        out, logs = attend(queries, keys, values, mask_ref[0])
        for which, value in enumerate((queries, keys, values)):
            put(qkv_ref, (3 * x + which) * PAIR, value)
        put(left_ref, x * (PAIR + ffn_n), out)
        put(log_ref, x * PAIR, logs)
    if len(layouts) > 1:
        backs = bind(layouts[1], weights)
        put_parts(z_ref, times(get(left_ref, 0, left_ref.shape[-1]), backs), *refs[8:10])


def slot_spec(width):
    return pl.BlockSpec((2, 1, HALF, width), lambda k: (0, k, 0, 0))


def fixed(shape):
    return pl.BlockSpec(
        shape, lambda *_: (0,) * len(shape), pipeline_mode=pl.Buffered(buffer_count=1)
    )


def slot_shape(width, kind):
    return jax.ShapeDtypeStruct((2, ZS, HALF, width), kind)


SMEM_SPEC = pl.BlockSpec(memory_space=pltpu.SMEM)
ANY_SPEC = pl.BlockSpec(memory_space=pl.ANY)
MASK_SPEC = pl.BlockSpec((1, ROWS, ROWS), lambda k: (k, 0, 0))
PART_SPEC = pl.BlockSpec((1, HALF, D), lambda k: (k, 0, 0))
PART_SHAPE = jax.ShapeDtypeStruct((ZS, HALF, D), BF)
ALL_ROWS = 2 * ZS * HALF
RELATIVE = pltpu.VMEM((ROWS, D), BF)


def front(z_array, rows, layouts, weights, bias, table, mask):
    n = bias.shape[1] // 2
    ffn_n = n - 3 * PAIR
    widths = [(D, BF), (6 * PAIR, BF), (2 * PAIR, F32), (2 * (PAIR + ffn_n), BF), (2 * ffn_n, BF)]
    parts = 2 * (len(layouts) - 1)
    return pl.pallas_call(
        lambda *refs: front_kernel(layouts, len(weights), *refs),
        grid=(ZS,),
        in_specs=[SMEM_SPEC]
        + [fixed(a.shape) for a in (*rows, *weights, bias)]
        + [slot_spec(3 * PAIR), MASK_SPEC],
        out_specs=[slot_spec(width) for width, _ in widths] + [PART_SPEC] * parts,
        out_shape=[slot_shape(*pair) for pair in widths] + [PART_SHAPE] * parts,
        scratch_shapes=[RELATIVE],
        compiler_params=pltpu.CompilerParams(vmem_limit_bytes=VMEM_LIMIT),
        cost_estimate=SMALL_COST,
        name="block_front",
    )(z_array, *rows, *weights, bias, table, mask)


def back_kernel(layout, z_ref, left_ref, *refs):
    left = get(left_ref, 0, left_ref.shape[-1])
    put_parts(z_ref, times(left, bind(layout, refs[:-2])), *refs[-2:])


def back(z_array, left, layout, weights):
    return pl.pallas_call(
        lambda *refs: back_kernel(layout, *refs),
        grid=(ZS,),
        in_specs=[SMEM_SPEC, slot_spec(left.shape[-1])] + [fixed(a.shape) for a in weights],
        out_specs=[PART_SPEC] * 2,
        out_shape=[PART_SHAPE] * 2,
        compiler_params=pltpu.CompilerParams(vmem_limit_bytes=VMEM_LIMIT),
        cost_estimate=SMALL_COST,
        name="block_back",
    )(z_array, left, *weights)


def reverse_kernel(layouts, count, z_ref, *refs):
    rows, refs = refs[:8], refs[8:]
    weights, refs = refs[:count], refs[count:]
    fronts, backs = [bind(layout, weights) for layout in layouts]
    slope_ref, qkv_ref, log_ref, table_ref, mask_ref = refs[:5]
    left_ref, own_ref, other_ref, sums_ref, relative = refs[5:]
    take_rows(z_ref, rows, relative)
    grad = relative[...]
    table = get(table_ref, 0, 3 * PAIR)
    n = fronts[0][2] - fronts[0][1]
    ffn_n = n - 3 * PAIR
    for x in range(2):
        both = times_t(grad, backs, x)
        gate = both[:, PAIR:] * get(slope_ref, x * ffn_n, ffn_n).astype(F32)
        put(left_ref, x * n + 3 * PAIR, gate)
        queries, keys, values = [get(qkv_ref, (3 * x + which) * PAIR, PAIR) for which in range(3)]
        grads = attend_back(
            queries, keys, values, get(log_ref, x * PAIR, PAIR), both[:, :PAIR].astype(BF), mask_ref[0]
        )
        grads = [turn_back(grads[0] * HEAD_DIM**-0.5, table), turn_back(grads[1], table), grads[2]]
        for which, value in enumerate(grads):
            put(left_ref, x * n + which * PAIR, value)
    left = get(left_ref, 0, left_ref.shape[-1])
    put_parts(z_ref, times(left, fronts), own_ref, other_ref)
    sums = jnp.sum(left.astype(F32), 0, keepdims=True)

    @pl.when(pl.program_id(0) == 0)
    def _():
        sums_ref[...] = sums

    @pl.when(pl.program_id(0) > 0)
    def _():
        sums_ref[...] += sums


def reverse(z_array, rows, layouts, weights, slope, qkv, logs, table, mask):
    _, first, last = layouts[0][0]
    n = last - first
    return pl.pallas_call(
        lambda *refs: reverse_kernel(layouts, len(weights), *refs),
        grid=(ZS,),
        in_specs=[SMEM_SPEC]
        + [fixed(a.shape) for a in (*rows, *weights)]
        + [slot_spec(a.shape[-1]) for a in (slope, qkv, logs, table)]
        + [MASK_SPEC],
        out_specs=[slot_spec(2 * n), PART_SPEC, PART_SPEC]
        + [pl.BlockSpec((1, 2 * n), lambda k: (0, 0))],
        out_shape=[slot_shape(2 * n, BF), PART_SHAPE, PART_SHAPE]
        + [jax.ShapeDtypeStruct((1, 2 * n), F32)],
        scratch_shapes=[RELATIVE],
        compiler_params=pltpu.CompilerParams(vmem_limit_bytes=VMEM_LIMIT),
        cost_estimate=SMALL_COST,
        name="block_reverse",
    )(z_array, *rows, *weights, slope, qkv, logs, table, mask)


def centred(hidden):
    centre = hidden - jnp.mean(hidden, -1, keepdims=True)
    rstd = lax.rsqrt(jnp.mean(centre * centre, -1, keepdims=True) + NORM_EPS)
    return centre * rstd, rstd


def model_row(ref, layer, which):
    return ref[layer * 4 + which : layer * 4 + which + 1].astype(F32)


def add_parts(refs):
    total = refs[0][...]
    for ref in refs[1:]:
        total = total + ref[...].astype(F32)
    return total


def norm_kernel(layer, final, hidden_ref, *refs):
    hidden = hidden_ref[...].astype(F32)
    parts, (model_ref, *outs) = refs[: len(refs) - 2 - (not final)], refs[len(refs) - 2 - (not final) :]
    if parts:
        bias = model_row(model_ref, layer - 1, 2) + model_row(model_ref, layer - 1, 3)
        hidden = hidden + add_parts(parts) + bias
    outs[0][...] = hidden.astype(outs[0].dtype)
    if not final:
        xhat, _ = centred(hidden)
        outs[1][...] = (
            xhat * model_row(model_ref, layer, 0) + model_row(model_ref, layer, 1)
        ).astype(BF)


def norm(layer, final, hidden, parts, model_vec):
    shapes = [jax.ShapeDtypeStruct((HALF, D), kind) for kind in ((BF,) if final else (F32, BF))]
    return pl.pallas_call(
        lambda *refs: norm_kernel(layer, final, *refs),
        out_shape=shapes,
        compiler_params=pltpu.CompilerParams(vmem_limit_bytes=VMEM_LIMIT),
        cost_estimate=SMALL_COST,
        name="norm",
    )(hidden, *parts, model_vec)


def norm_back_kernel(layer, count, grad_ref, hidden_ref, *refs):
    parts, model_ref, (next_ref, low_ref, sums_ref) = refs[:count], refs[count], refs[-3:]
    grad_next = grad_ref[...].astype(F32)
    grad_normed = add_parts(parts)
    xhat, rstd = centred(hidden_ref[...].astype(F32))
    sums_ref[...] = jnp.concatenate(
        [
            jnp.sum(grad_normed * xhat, 0, keepdims=True),
            jnp.sum(grad_normed, 0, keepdims=True),
            jnp.sum(grad_next, 0, keepdims=True),
            jnp.zeros((5, grad_next.shape[1]), F32),
        ],
        0,
    )
    scaled = grad_normed * model_row(model_ref, layer, 0)
    grad = grad_next + rstd * (
        scaled
        - jnp.mean(scaled, -1, keepdims=True)
        - xhat * jnp.mean(scaled * xhat, -1, keepdims=True)
    )
    next_ref[...] = grad
    low_ref[...] = grad.astype(BF)


def norm_back(layer, grad_next, hidden, parts, model_vec, earlier=()):
    vmem = pl.BlockSpec(memory_space=pltpu.VMEM)
    return pl.pallas_call(
        lambda *refs: norm_back_kernel(layer, len(parts), *refs),
        in_specs=[vmem] * (3 + len(parts)) + [ANY_SPEC] * len(earlier),
        out_shape=[
            jax.ShapeDtypeStruct((HALF, D), F32),
            jax.ShapeDtypeStruct((HALF, D), BF),
            jax.ShapeDtypeStruct((8, D), F32),
        ],
        compiler_params=pltpu.CompilerParams(vmem_limit_bytes=VMEM_LIMIT),
        cost_estimate=SMALL_COST,
        name="norm_back",
    )(grad_next, hidden, *parts, model_vec, *earlier)


def fold_kernel(count, z_ref, own_ref, other_ref, *refs):
    outs = refs[len(refs) - count :]
    totals = [own_ref[k].astype(F32) + other_ref[k].astype(F32) for k in range(ZS)]
    for k in range(ZS):
        outs[k][...] = totals[k].astype(outs[k].dtype)
    if len(outs) > ZS:
        outs[ZS][...] = jnp.where(z_ref[0] == 0, totals[1], totals[3]).astype(BF)


def fold(z_array, own, other, kinds, earlier=()):
    return pl.pallas_call(
        lambda *refs: fold_kernel(len(kinds), *refs),
        in_specs=[pl.BlockSpec(memory_space=pltpu.SMEM)]
        + [pl.BlockSpec(memory_space=pltpu.VMEM)] * 2
        + [ANY_SPEC] * len(earlier),
        out_shape=[jax.ShapeDtypeStruct((HALF, D), kind) for kind in kinds],
        compiler_params=pltpu.CompilerParams(vmem_limit_bytes=VMEM_LIMIT),
        cost_estimate=SMALL_COST,
        name="fold",
    )(z_array, own, other, *earlier)


class Place:
    def __init__(self, ny):
        self.ny = ny
        self.z = lax.axis_index("z")
        self.y = lax.axis_index("y")
        self.x = lax.axis_index("x")
        self.c = lax.axis_index("c")

    def own_first(self, lower, upper, index, axis):
        mine = jnp.where(index == 0, lower, upper)
        other = jnp.where(index == 0, upper, lower)
        return jnp.concatenate([mine, other], axis)

    def to_local(self, array):
        parts = array.reshape(*array.shape[:-1], ZS, self.ny, -1)
        parts = jnp.swapaxes(parts, -2, -3).reshape(*array.shape[:-1], 2, -1)
        lower, upper = parts[..., 0, :], parts[..., 1, :]
        if self.ny == 2:
            return self.own_first(lower, upper, self.y, -1)
        return jnp.concatenate([lower, upper], -1)

    def from_local(self, array):
        half = array.shape[-1] // 2
        lower, upper = array[..., :half], array[..., half:]
        if self.ny == 2:
            array = self.own_first(lower, upper, self.y, -1)
        parts = array.reshape(*array.shape[:-1], self.ny, ZS, -1)
        return jnp.swapaxes(parts, -2, -3).reshape(*array.shape)

    def y_columns(self, array):
        if self.ny == 2:
            return jnp.concatenate([array, swap(array, "y")], -1)
        return lax.all_gather(array, "y", axis=array.ndim - 1, tiled=True)

    def y_place(self, array):
        if self.ny == 2:
            other = swap(array, "y")
            return self.own_first(array, other, self.y, -1)
        return lax.all_gather(array, "y", axis=array.ndim - 1, tiled=True)


def after(array, *earlier):
    return lax.optimization_barrier((array, *earlier))[0]


def gather_z(array):
    return [array] + [shift_z(array, k) for k in range(1, ZS)]


def line_z(array, pairs):
    return lax.ppermute(array, "z", pairs)


def gather_rows(rows, *earlier):
    mine = gather_z(rows)
    return mine + [swap(after(part, *earlier) if earlier else part, "c") for part in mine]


def gather_line(place, rows, *deadlines, second=()):
    far = swap(rows, "c")
    up_one = line_z(rows, [(0, 1), (1, 2), (2, 3)])
    down_one = line_z(rows, [(3, 2), (2, 1), (1, 0)])
    up_one, down_one = after(up_one, far, *second), after(down_one, *second)
    up_two = line_z(up_one, [(1, 2), (2, 3)])
    down_two = line_z(down_one, [(2, 1), (1, 0)])
    two = up_two + down_two
    if deadlines:
        two = after(two, *deadlines)
    far_two = swap(two, "c")
    end = after(line_z(two, [(2, 3), (1, 0)]), far_two)
    one = jnp.where(place.z == 0, end, up_one)
    three = jnp.where(place.z == ZS - 1, end, down_one)
    return [rows, one, two, three, far, swap(one, "c"), far_two, swap(three, "c")]


def scatter_rows(z_array, parts, *earlier):
    own, other = parts
    if earlier:
        other = after(other, *earlier)
    terms = fold(z_array, own, swap(other, "c"), (F32, BF, BF, BF))
    return [terms[0]] + [shift_z(terms[k], -k) for k in range(1, ZS)]


def scatter_line(z_array, parts, first=(), then=(), mid=(), last=(), tokens=()):
    own, other = parts
    if first:
        other = after(other, *first)
    other = swap(other, "c")
    if then:
        other = after(other, *then)
    own, one, two, three, end = fold(z_array, own, other, (F32, F32, F32, F32, BF), tokens)
    end = line_z(end, [(0, 1), (3, 2)])
    two = (two + end.astype(F32)).astype(BF)
    if mid:
        two = after(two, *mid)
    down_two = line_z(two, [(2, 1), (3, 2)])
    up_two = line_z(two, [(1, 2), (0, 1)])
    one = (one + down_two.astype(F32)).astype(BF)
    three = (three + up_two.astype(F32)).astype(BF)
    if last:
        one, three = after(one, *last), after(three, *last)
    down_one = line_z(one, [(1, 0), (2, 1), (3, 2)])
    up_one = line_z(three, [(0, 1), (1, 2), (2, 3)])
    return [own, down_one, up_one]


def whole_spec(shape):
    return pl.BlockSpec(shape, lambda *_: (0,) * len(shape))


def quarter(z_ref, k, sign):
    return (z_ref[0] + sign * k + ZS) % ZS


def weight_specs(kind, layer, dd, heads_n, ffn_n, sign):
    fronts = [
        pl.BlockSpec((1, 3, dd, heads_n), lambda k, z: (layer, 0, 0, quarter(z, k, sign))),
        pl.BlockSpec((1, dd, ffn_n), lambda k, z: (layer, 0, quarter(z, k, sign))),
    ]
    backs = [
        pl.BlockSpec((1, heads_n, dd), lambda k, z: (layer, quarter(z, k, sign), 0)),
        pl.BlockSpec((1, ffn_n, dd), lambda k, z: (layer, quarter(z, k, sign), 0)),
    ]
    return {"front": fronts, "back": backs, "both": fronts + backs}[kind]


def pack_kernel(kind, z_ref, *refs):
    refs, outs = refs[:-ZS], refs[-ZS:]
    parts = []
    if kind != "back":
        parts += [refs[0][0, which].T for which in range(3)] + [refs[1][0].T]
    if kind != "front":
        parts += [refs[-2][0], refs[-1][0]]
    block = jnp.concatenate(parts, 0).astype(BF)
    for k in range(ZS):

        @pl.when(pl.program_id(0) == k)
        def _():
            outs[k][...] = block


def pack(kind, layer, z_array, arrays, dd, heads_n, ffn_n):
    n = {"front": 3 * heads_n + ffn_n, "back": heads_n + ffn_n, "both": 4 * heads_n + 2 * ffn_n}[kind]
    return pl.pallas_call(
        lambda *refs: pack_kernel(kind, *refs),
        grid_spec=pltpu.PrefetchScalarGridSpec(
            num_scalar_prefetch=1,
            grid=(ZS,),
            in_specs=weight_specs(kind, layer, dd, heads_n, ffn_n, 1),
            out_specs=[whole_spec((n, dd))] * ZS,
        ),
        out_shape=[jax.ShapeDtypeStruct((n, dd), BF)] * ZS,
        compiler_params=pltpu.CompilerParams(vmem_limit_bytes=VMEM_LIMIT),
        cost_estimate=pl.CostEstimate(
            flops=0, bytes_accessed=6 * ZS * n * dd, transcendentals=0
        ),
        name="pack_" + kind,
    )(z_array, *arrays)


def stack_kernel(*refs):
    dd = refs[0].shape[1]
    for at, ref in enumerate(refs[:-1]):
        refs[-1][:, at * dd : (at + 1) * dd] = ref[...]


def stack(pieces):
    n, dd = pieces[0].shape
    if dd % 128:
        return jnp.concatenate(pieces, 1)
    return pl.pallas_call(
        stack_kernel,
        out_shape=jax.ShapeDtypeStruct((n, len(pieces) * dd), BF),
        compiler_params=pltpu.CompilerParams(vmem_limit_bytes=VMEM_LIMIT),
        cost_estimate=SMALL_COST,
        name="stack",
    )(*pieces)


def stack_rows_kernel(*refs):
    for at, ref in enumerate(refs[:-1]):
        refs[-1][at * HALF : (at + 1) * HALF] = ref[...]


def stack_rows(rows):
    return pl.pallas_call(
        stack_rows_kernel,
        out_shape=jax.ShapeDtypeStruct((len(rows) * HALF, D), BF),
        compiler_params=pltpu.CompilerParams(vmem_limit_bytes=VMEM_LIMIT),
        cost_estimate=SMALL_COST,
        name="stack_rows",
    )(*rows)


def spread_xy(kind, near, *earlier):
    cut = cut_of(kind)
    on_x, on_y = swap(near, "x"), swap(near, "y")
    one, two = on_x[:cut], on_y[cut:]
    if earlier:
        one, two = after(one, *earlier), after(two, *earlier)
    return near, on_y, on_x, swap(one, "y"), swap(two, "x")


def weight_grads(kind, left, right, cut):
    n, half = left.shape[1] // 2, right.shape[1] // 2
    cut = min(cut, n)
    lower, upper = right[:, :half], right[:, half:]
    own, other = left[:, :n], left[:, n:]
    return [
        dot_tn(one, two).astype(BF) if one.shape[1] else jnp.zeros((0, half), BF)
        for one, two in (
            (other[:, :cut], upper),
            (other[:, cut:], upper),
            (own, upper),
            (other, lower),
            (own, lower),
        )
    ]


def bump_kernel(count, *refs):
    parts, (one_ref, two_ref), (y_ref, x_ref) = refs[: 2 * count], refs[2 * count :][:2], refs[-2:]
    at = 0
    for on_y, on_x in zip(parts[:count], parts[count:]):
        rows = slice(at, at + on_y.shape[0])
        y_ref[rows] = on_y[...]
        x_ref[rows] = on_x[...]
        at += on_y.shape[0]
    cut = one_ref.shape[0]
    y_ref[:cut] = add_low(y_ref[:cut], one_ref[...])
    x_ref[cut:] = add_low(x_ref[cut:], two_ref[...])


def bump(on_y, on_x, far_one, far_two, earlier=()):
    n = sum(part.shape[0] for part in on_y)
    vmem = pl.BlockSpec(memory_space=pltpu.VMEM)
    return pl.pallas_call(
        lambda *refs: bump_kernel(len(on_y), *refs),
        in_specs=[vmem] * (2 * len(on_y) + 2) + [ANY_SPEC] * len(earlier),
        out_shape=[jax.ShapeDtypeStruct((n, on_y[0].shape[1]), BF)] * 2,
        compiler_params=pltpu.CompilerParams(vmem_limit_bytes=VMEM_LIMIT),
        cost_estimate=SMALL_COST,
        name="bump",
    )(*on_y, *on_x, far_one, far_two, *earlier)


def split_kernel(count, z_ref, *refs):
    near, (y_ref, x_ref, *_), outs = refs[:count], refs[count:], refs[-ZS:]
    value = jnp.concatenate([part[...] for part in near], 0).astype(F32)
    value = (value + y_ref[...].astype(F32) + x_ref[...].astype(F32)).astype(BF)
    for k in range(ZS):

        @pl.when(pl.program_id(0) == k)
        def _():
            outs[k][...] = value


def split(z_array, near, from_y, from_x, earlier=()):
    n, width = from_y.shape
    dd = width // ZS
    return pl.pallas_call(
        lambda *refs: split_kernel(len(near), *refs),
        grid_spec=pltpu.PrefetchScalarGridSpec(
            num_scalar_prefetch=1,
            grid=(ZS,),
            in_specs=[
                pl.BlockSpec((part.shape[0], dd), lambda k, z: (0, quarter(z, k, 1)))
                for part in (*near, from_y, from_x)
            ]
            + [ANY_SPEC] * len(earlier),
            out_specs=[whole_spec((n, dd))] * ZS,
        ),
        out_shape=[jax.ShapeDtypeStruct((n, dd), BF)] * ZS,
        compiler_params=pltpu.CompilerParams(vmem_limit_bytes=VMEM_LIMIT),
        cost_estimate=SMALL_COST,
        name="split",
    )(z_array, *near, from_y, from_x, *earlier)


def add_low(left, right):
    return (left.astype(F32) + right.astype(F32)).astype(BF)


def sum_plain(place, grads):
    own = jnp.concatenate([jnp.concatenate([g[4], g[2]], 1) for g in grads], 0)
    other = [jnp.concatenate([g[3], jnp.concatenate([g[0], g[1]], 0)], 1) for g in grads]
    both = add_low(own, swap(jnp.concatenate(other, 0), "x"))
    total = lax.psum_scatter(both, "y", scatter_dimension=1, tiled=True)
    n, width = total.shape
    dd = width // ZS
    return [lax.dynamic_slice(total, (0, (place.z + k) % ZS * dd), (n, dd)) for k in range(ZS)]


def adam_kernel(kind, heads_n, ffn_n, offset, rates, z_ref, *refs):
    pieces, states, outs = refs[:ZS], refs[ZS : ZS + 6], refs[-9:-1]
    refs[-1][...] = jnp.zeros_like(refs[-1])
    for k in range(ZS):

        @pl.when(pl.program_id(0) == k)
        def _():
            split = (3 if kind == "front" else 1) * heads_n
            piece = pieces[k][offset : offset + split + ffn_n]
            if kind == "front":
                grads = [
                    jnp.stack(
                        [
                            piece[which * heads_n : (which + 1) * heads_n].astype(F32).T
                            for which in range(3)
                        ]
                    )[None],
                    piece[split:].astype(F32).T[None],
                ]
            else:
                grads = [piece[:split].astype(F32)[None], piece[split:].astype(F32)[None]]
            for at, grad in enumerate(grads):
                weight, first, second = [ref[...] for ref in states[at * 3 : at * 3 + 3]]
                outs[at * 4][...] = grad
                new = adamw(weight, grad, first, second, rates[at], DECAY)
                for ref, value in zip(outs[at * 4 + 1 : at * 4 + 4], new):
                    ref[...] = value


def adam(kind, layer, z_array, pieces, offset, states, rates, earlier, tokens, heads_n, ffn_n):
    n, dd = pieces[0].shape
    first, second = weight_specs(kind, layer, dd, heads_n, ffn_n, -1)
    shapes = [jax.ShapeDtypeStruct(states[at].shape, F32) for at in (0, 3) for _ in range(4)]
    earlier = list(earlier or [])
    return pl.pallas_call(
        lambda *refs: adam_kernel(kind, heads_n, ffn_n, offset, rates, *refs),
        grid_spec=pltpu.PrefetchScalarGridSpec(
            num_scalar_prefetch=1,
            grid=(ZS,),
            in_specs=[whole_spec((n, dd))] * ZS
            + [first] * 3
            + [second] * 3
            + [ANY_SPEC] * (len(earlier) + len(tokens)),
            out_specs=[first] * 4 + [second] * 4 + [whole_spec((8, 128))],
        ),
        out_shape=shapes + [jax.ShapeDtypeStruct((8, 128), F32)],
        input_output_aliases={1 + ZS + 6 + at: at for at in range(len(earlier))},
        compiler_params=pltpu.CompilerParams(vmem_limit_bytes=VMEM_LIMIT),
        cost_estimate=SMALL_COST,
        name="adam_" + kind,
    )(z_array, *pieces, *states, *earlier, *tokens)


def tables(positions):
    half = ROT // 2
    places = jnp.maximum(positions, 0).astype(F32)
    frequency = 10000.0 ** (-(2.0 / ROT) * jnp.arange(half).astype(F32))
    angles = places[..., None] * frequency
    both = jnp.concatenate([jnp.cos(angles), jnp.sin(angles)], -1)
    pick = np.zeros((ROT, 3, 2, HEAD_DIM), np.float32)
    for at in range(half):
        pick[at, 0, :, at] = pick[at, 0, :, half + at] = 1.0
        pick[half + at, 1, :, at] = -1.0
        pick[half + at, 2, :, half + at] = 1.0
    rest = np.zeros((3, 2, HEAD_DIM), np.float32)
    rest[0, :, ROT:] = 1.0
    table = jnp.dot(both, pick.reshape(ROT, -1), precision=lax.Precision.HIGHEST)
    return table + rest.reshape(-1)


def adamw(weight, grad, first, second, rate, decay):
    first_new = BETA_ONE * first + (1.0 - BETA_ONE) * grad
    second_new = BETA_TWO * second + (1.0 - BETA_TWO) * grad * grad
    first_hat = first_new / (1.0 - BETA_ONE**STEP)
    second_hat = second_new / (1.0 - BETA_TWO**STEP)
    weight_new = weight - rate * (first_hat / (jnp.sqrt(second_hat) + ADAM_EPS) + decay * weight)
    return (first_new, second_new, weight_new)


def source_lane(at, y):
    return (at % ZS) * 2 + (at // ZS + y) % 2


def take_kernel(place_ref, rows_ref, grads_ref, live_ref, start_ref, low_ref):
    dd = D // (2 * ZS)
    for at in range(2 * ZS):
        lanes = pl.ds(pl.multiple_of(source_lane(at, place_ref[1]) * dd, 128), dd)
        to = slice(at * dd, (at + 1) * dd)
        start_ref[:, to] = rows_ref[:, lanes]
        low_ref[:, to] = (grads_ref[:, lanes].astype(F32) * live_ref[...]).astype(BF)


def take(place, activations, cotangent, live):
    m = place.x * 2 + place.c
    if place.ny != 2:
        mine = [
            place.to_local(lax.dynamic_slice_in_dim(array, m * HALF, HALF, 0))
            for array in (activations, cotangent)
        ]
        return mine[0], (mine[1].astype(F32) * live).astype(BF)
    where = jnp.stack([m, place.y]).astype(jnp.int32)
    return pl.pallas_call(
        take_kernel,
        grid_spec=pltpu.PrefetchScalarGridSpec(
            num_scalar_prefetch=1,
            grid=(1,),
            in_specs=[pl.BlockSpec((HALF, D), lambda at, ref: (ref[0], 0))] * 2
            + [pl.BlockSpec((HALF, 1), lambda at, ref: (0, 0))],
            out_specs=[pl.BlockSpec((HALF, D), lambda at, ref: (0, 0))] * 2,
        ),
        out_shape=[jax.ShapeDtypeStruct((HALF, D), BF)] * 2,
        cost_estimate=pl.CostEstimate(flops=0, bytes_accessed=8 * HALF * D, transcendentals=0),
        name="take",
    )(where, activations, cotangent, live)


def give_kernel(place_ref, *refs):
    dd = D // (2 * ZS)
    for block in range(4):

        @pl.when(pl.program_id(0) == block)
        def _():
            for at in range(2 * ZS):
                lanes = pl.ds(pl.multiple_of(source_lane(at, place_ref[2]) * dd, 128), dd)
                refs[-1][:, lanes] = refs[block][:, at * dd : (at + 1) * dd].astype(F32)


def give(place, blocks):
    where = jnp.stack([place.x, place.c, place.y]).astype(jnp.int32)
    if place.ny != 2:
        result = jnp.zeros((4 * HALF, D), F32)
        for at, block in enumerate(blocks):
            row = ((place.x + at // 2) % 2) * 2 + (place.c + at % 2) % 2
            result = lax.dynamic_update_slice(
                result, place.from_local(block).astype(F32), (row * HALF, 0)
            )
        return result

    def target(at, ref):
        return (((ref[0] + at // 2) % 2) * 2 + (ref[1] + at % 2) % 2, 0)

    return pl.pallas_call(
        give_kernel,
        grid_spec=pltpu.PrefetchScalarGridSpec(
            num_scalar_prefetch=1,
            grid=(4,),
            in_specs=[whole_spec((HALF, D))] * 4,
            out_specs=pl.BlockSpec((HALF, D), target),
        ),
        out_shape=jax.ShapeDtypeStruct((4 * HALF, D), F32),
        compiler_params=pltpu.CompilerParams(vmem_limit_bytes=VMEM_LIMIT),
        cost_estimate=SMALL_COST,
        name="give",
    )(where, *blocks)


def per_device(
    ny,
    activations,
    cotangent,
    positions,
    w_qkv,
    w_out,
    w_up,
    w_down,
    vec_model,
    vec_head,
    vec_ffn,
    first_qkv,
    first_out,
    first_up,
    first_down,
    first_model,
    first_head,
    first_ffn,
    second_qkv,
    second_out,
    second_up,
    second_down,
    second_model,
    second_head,
    second_ffn,
):
    place = Place(ny)
    dd = w_up.shape[1]
    heads_n = w_qkv.shape[3] // ZS
    ffn_n = w_up.shape[2] // ZS
    sizes = (dd, heads_n, ffn_n)
    z_array = place.z.reshape(1).astype(jnp.int32)

    model_own = vec_model.astype(BF).reshape(LAYERS * 4, dd)
    head_own, ffn_own = vec_head.astype(BF), vec_ffn.astype(BF)
    if ny == 2:
        first = jnp.concatenate(
            [model_own.reshape(-1), head_own.reshape(-1), ffn_own.reshape(-1)]
        )
        far = swap(first, "y")
        ends = [model_own.size, model_own.size + head_own.size, first.size]
        model_far, head_far, ffn_far = [
            far[start:end].reshape(own.shape)
            for start, end, own in zip([0] + ends, ends, (model_own, head_own, ffn_own))
        ]
        model_y = jnp.stack([model_own, model_far], 1)
        head_y = place.own_first(head_own, head_far, place.y, -1)
        ffn_y = place.own_first(ffn_own, ffn_far, place.y, -1)
    else:
        model_y = lax.all_gather(model_own, "y", axis=1)
        head_y = lax.all_gather(head_own, "y", axis=2, tiled=True)
        ffn_y = lax.all_gather(ffn_own, "y", axis=1, tiled=True)
    slim = jnp.concatenate([head_y.reshape(LAYERS, -1), ffn_y], 1)
    places_x = lax.dynamic_slice_in_dim(positions, place.x * ROWS, ROWS)
    places_x = place.own_first(places_x[:HALF], places_x[HALF:], place.c, 0)
    if ny == 2:
        pieces_front = pack("front", 0, z_array, (w_qkv, w_up), *sizes)
        slim = after(slim, *pieces_front)
    mine = jnp.concatenate([model_y.reshape(-1), places_x.astype(BF)])
    slim_x = swap(slim, "x")
    bias = jnp.concatenate([slim, slim_x], 1).astype(F32)
    packed = jnp.stack(
        [mine] + [lax.ppermute(mine, "z", [(i, i ^ k) for i in range(ZS)]) for k in range(1, ZS)]
    )
    if ny == 2:
        pieces_front = [after(piece, packed, slim_x) for piece in pieces_front]
        came_front = [pieces_front[0]] + [shift_z(pieces_front[k], k) for k in range(1, ZS)]
        on_x, on_y = swap(pieces_front[0], "x"), swap(pieces_front[0], "y")
        later_z = after(z_array, on_x, on_y)
        pieces_next = pack("both", 1, later_z, (w_qkv, w_up, w_out, w_down), *sizes)
        pieces_back = pack("back", 0, later_z, (w_out, w_down), *sizes)
        cut = cut_of("front")
        ready = *pieces_next, *pieces_back
        far_one, far_two = after(on_x[:cut], *ready), after(on_y[cut:], *ready)
        own_front = pieces_front[0], on_y, on_x, swap(far_one, "y"), swap(far_two, "x")
    everyone = jnp.arange(ZS, dtype=jnp.int32)
    by_z = jnp.take(packed, everyone ^ place.z, axis=0)
    model_vec = by_z[:, : LAYERS * 4 * ny * dd].reshape(ZS, LAYERS * 4, ny, dd)
    model_vec = model_vec.transpose(1, 2, 0, 3).reshape(LAYERS * 4, D)
    places = jnp.take(by_z[:, LAYERS * 4 * ny * dd :], (place.z - everyone) % ZS, axis=0)
    places = places.astype(F32).astype(jnp.int32)

    order = (jnp.arange(ROWS, dtype=jnp.int32) + place.c * HALF) % ROWS
    starts = order - jnp.maximum(places, 0)
    seen = (order[None, None, :] <= order[None, :, None]) & (
        order[None, None, :] >= starts[:, :, None]
    )
    mask = jnp.where(seen, 0.0, MASKED).astype(F32)
    table = tables(jnp.swapaxes(places.reshape(ZS, 2, HALF), 0, 1))

    mine = place.x * ROWS + place.c * HALF
    live = (lax.dynamic_slice_in_dim(positions, mine, HALF) >= 0).astype(F32)[:, None]
    if ny == 2:
        live = after(live, *own_front[1:3])
    start, last_low = take(place, activations, cotangent, live)

    kernel_z = z_array if ny == 2 else jnp.zeros_like(z_array)
    n_front, n_back = 3 * heads_n + ffn_n, heads_n + ffn_n
    n_both = n_front + n_back
    arrays = {"front": (w_qkv, w_up), "back": (w_out, w_down), "both": (w_qkv, w_up, w_out, w_down)}

    def packed_pieces(kind, layer):
        return pack(kind, layer, z_array, arrays[kind], *sizes)

    def send_z(pieces, *earlier):
        if earlier:
            pieces = [pieces[0]] + [after(piece, *earlier) for piece in pieces[1:]]
        return [pieces[0]] + [shift_z(pieces[k], k) for k in range(1, ZS)]

    def spread_plain(kind, layer):
        pieces = send_z(packed_pieces(kind, layer))
        n = pieces[0].shape[0]
        joined = jnp.zeros((n, ZS * dd), BF)
        for k, piece in enumerate(pieces):
            joined = lax.dynamic_update_slice(joined, piece, (0, (place.z - k) % ZS * dd))
        own = place.y_columns(joined).reshape(n, 2, ZS, -1)
        own = jnp.stack([own[:, :, -k % ZS] for k in ORDER], 2).reshape(n, D)
        other = swap(own, "x")
        cut, half = cut_of(kind), D // 2
        return own[:, :half], own[:, half:], other[:, :half], other[:cut, half:], other[cut:, half:]

    def layout_of(kind, chunks, first=0):
        n, cut = {"front": n_front, "back": n_back}[kind], cut_of(kind)
        ids = [tuple(5 * c + at for c in range(chunks)) for at in range(5)]
        far = [(ids[3], 0, cut), (ids[4], 0, n - cut)]
        return (*((ids[at], 0, n) for at in range(3)), far)

    both_cut = cut_of("both")
    chunks = 3 if ny == 2 else 1
    ids = [tuple(5 * c + at for c in range(chunks)) for at in range(5)]
    merged = (
        (*((ids[at], 0, n_front) for at in range(3)), [(ids[3], 0, both_cut), (ids[4], 0, n_front - both_cut)]),
        (*((ids[at], n_front, n_both) for at in range(3)), [(ids[4], n_front - both_cut, n_both - both_cut)]),
    )

    hidden, normed = norm(0, False, start, (), model_vec)
    if ny == 2:
        came_front[1] = after(came_front[1], start)
        came_back = send_z(pieces_back, *came_front[1:])
        rest_front = list(
            spread_xy("front", stack([after(came_front[1], *own_front[3:]), *came_front[:1:-1]]))
        )
        fronts = [*own_front, *rest_front]
        rest_front[1] = after(rest_front[1], table, mask)
        near_back = stack([came_back[0], after(came_back[1], *rest_front[3:]), *came_back[:1:-1]])
        on_x, on_y = swap(near_back, "x"), swap(near_back, "y")
        rows = gather_line(
            place, after(normed, *came_back[1:]), near_back, second=rest_front[1:3]
        )
        came_next = send_z(pieces_next, *rows[1:4])
    else:
        rows = gather_line(place, normed)
        fronts = spread_plain("front", 0)
        backs = spread_plain("back", 0)
    layouts = layout_of("front", 2 if ny == 2 else 1), layout_of("back", 1)
    shift = len(fronts)
    move = lambda part: (tuple(at + shift for at in part[0]), *part[1:])
    joint = layouts[0], (*map(move, layouts[1][:3]), [move(part) for part in layouts[1][3]])

    normed, qkv, logs, left, slope = front(
        kernel_z, rows, layouts[:1], fronts, bias[0:1], table, mask
    )
    kept = [(hidden, normed, qkv, logs, left, slope)]
    if ny == 2:
        cut, ready = cut_of("back"), (left, came_next[1], came_next[3])
        far_one, far_two = after(on_x[:cut], *ready), after(on_y[cut:], *ready)
        backs = near_back, on_y, on_x, swap(far_one, "y"), swap(far_two, "x")
        first_next = spread_xy("both", after(came_next[0], *backs[3:]))
        mid_next = stack([came_next[1], came_next[3]])
        left = after(left, mid_next)
    own, other = back(kernel_z, left, layouts[1], backs)
    if ny == 2:
        last_piece = after(came_next[2], other)
        mid_next = spread_xy("both", after(mid_next, *first_next[1:3]))
        last_next = spread_xy("both", after(last_piece, *mid_next[1:3]))
        spread = [*first_next, *mid_next, *last_next]
        parts = scatter_line(z_array, (own, other), first=(last_piece, *first_next[1:3]))
        parts[2] = after(parts[2], *mid_next[1:3], *first_next[3:])
    else:
        spread = spread_plain("both", 1)
        parts = scatter_line(z_array, (own, other))
    hidden, normed = norm(1, False, hidden, parts, model_vec)
    if ny == 2:
        rows = gather_line(place, normed, second=(*last_next[1:3], *mid_next[3:]))
    else:
        rows = gather_line(place, normed)
    mine_z = rows[1:4]
    normed, qkv, logs, left, slope, own, other = front(
        kernel_z, rows, merged, spread, bias[1:2], table, mask
    )
    kept.append((hidden, normed, qkv, logs, left, slope))
    rows = gather_rows(after(last_low, *mine_z))
    rest = scatter_rows(z_array, (own, other), *rows[1:4])
    rows[4] = after(rows[4], rest[0])

    outs = {"front": None, "back": None}
    states = {
        "front": (w_qkv, first_qkv, second_qkv, w_up, first_up, second_up),
        "back": (w_out, first_out, second_out, w_down, first_down, second_down),
    }
    rate_in = 3.0 / math.sqrt(D)
    rates = {
        "front": (rate_in, rate_in),
        "back": (12.0 / math.sqrt(D), 3.0 / math.sqrt(FF)),
    }

    def flat(array):
        return array.reshape(ALL_ROWS, -1)

    def first_hop(grads, earlier=()):
        far_one = jnp.concatenate([g[0] for g in grads], 0) if len(grads) > 1 else grads[0][0]
        far_two = jnp.concatenate([g[1] for g in grads], 0) if len(grads) > 1 else grads[0][1]
        return bump(
            [g[2] for g in grads],
            [g[3] for g in grads],
            swap(far_one, "x"),
            swap(far_two, "y"),
            earlier,
        )

    def second_hop(on_y, on_x):
        return swap(on_y, "y"), swap(on_x, "x")

    def step(kind, layer, pieces, offset, tokens=()):
        *outs[kind], token = adam(
            kind, layer, z_array, pieces, offset, states[kind], rates[kind], outs[kind], tokens, heads_n, ffn_n
        )
        return token

    sums, slims = {}, {}
    hidden_in, normed, qkv, logs, left, slope = kept[1]
    left_grad, own, other, slims[1] = reverse(
        kernel_z, rows, merged, spread, slope, qkv, logs, table, mask
    )
    grads = [
        weight_grads("back", flat(left), stack_rows(rows), cut_of("back")),
        weight_grads("front", flat(left_grad), flat(normed), cut_of("front")),
    ]
    (result,) = norm(LAYERS, True, hidden, rest, model_vec)
    result_x = swap(result, "x")
    results = [result, swap(result, "c"), result_x, swap(result_x, "c")]
    if ny == 2:
        hops = [first_hop(grads[:1])]
        seconds = [second_hop(*hops[0])]
        parts = scatter_line(z_array, (own, other), rest[1:], last=(*hops[0], result_x))
        late_far = [after(part, *seconds[0], *parts[1:]) for part in grads[1][:2]]
        hops.append(first_hop([late_far + grads[1][2:]]))
        grad_next, low, sums[1] = norm_back(1, last_low, hidden_in, parts, model_vec)
        seconds.append(second_hop(*hops[1]))
        rows = gather_line(place, low, *hops[1], second=(results[1], results[3]))
        came_one = [send_z(split(z_array, grads[0][4:], *seconds[0]), *rows[5:]), None]
    else:
        parts = scatter_line(z_array, (own, other))
        grad_next, low, sums[1] = norm_back(1, last_low, hidden_in, parts, model_vec)
        rows = gather_line(place, low)
        came_one = [send_z(sum_plain(place, grads[:1])), sum_plain(place, grads[1:])]
    hidden_in, normed, qkv, logs, left, slope = kept[0]
    left_grad, own, other, slims[0] = reverse(
        kernel_z, rows, joint, [*fronts, *backs], slope, qkv, logs, table, mask
    )
    left_grad = after(left_grad, *came_one[0][1:])
    if ny == 2:
        came_one[1] = split(z_array, grads[1][4:], *seconds[1], [slims[0]])
    grads_front = weight_grads("front", flat(left_grad), flat(normed), cut_of("front"))
    came_one[1] = send_z(came_one[1], *came_one[0][1:])
    if ny == 2:
        hop_front = first_hop([grads_front])
        second_front = second_hop(*hop_front)
        rows = [after(row, hop_front[0]) for row in rows]
    grads_back = weight_grads("back", flat(left), stack_rows(rows), cut_of("back"))
    result_rows = give(place, results)
    if ny == 2:
        parts = scatter_line(
            z_array,
            (own, other),
            (came_one[1][1], came_one[1][3], *hop_front),
            came_one[1][2:3],
            second_front,
        )
        near_front = after(grads_front[4], *grads_back[:2])
        sum_front = split(z_array, [near_front], *second_front)
        came_front = send_z(sum_front)
        late_far = [after(part, *second_front) for part in grads_back[:2]]
        hop_back = first_hop([late_far + grads_back[2:]])
        second_back = second_hop(*(after(p, came_front[1], came_front[3]) for p in hop_back))
        sum_back = split(z_array, grads_back[4:], *second_back, [result_rows])
        came_back = send_z(sum_back)
        norm_parts = [*parts[:2], after(parts[2], *came_front[1:], *second_back)]
    else:
        parts = scatter_line(z_array, (own, other))
        came_front = send_z(sum_plain(place, [grads_front]))
        sum_back = sum_plain(place, [grads_back])
        came_back = send_z(sum_back)
        norm_parts = parts
    grad_next, low, sums[0] = norm_back(0, grad_next, hidden_in, norm_parts, model_vec)
    came_one = [[after(piece, sum_back[0]) for piece in pieces] for pieces in came_one]
    came_front = [after(piece, sum_back[0]) for piece in came_front]
    step("back", 1, came_one[0], 0)
    step("front", 1, came_one[1], 0)
    token = step("front", 0, came_front, 0)
    step("back", 0, came_back, 0, [token])
    late = sum_back[0]

    low_x = swap(low, "x")
    low, low_x = [after(part, *came_back[1:]) for part in (low, low_x)]
    both = after(jnp.concatenate([slims[0], slims[1]], 0), late)
    n = both.shape[1] // 2
    slim = both[:, :n] + swap(both[:, n:], "x")
    heads = slim[:, : 3 * heads_n].reshape(LAYERS, 3, ny, -1)
    ffns = slim[:, 3 * heads_n :].reshape(LAYERS, ny, -1)
    slim = jnp.concatenate([heads.swapaxes(1, 2).reshape(LAYERS, ny, -1), ffns], 2)
    if ny == 2:
        mine, far = [jnp.where(place.y == at, slim[:, 0], slim[:, 1]) for at in range(2)]
        slim = mine + swap(far, "y")
    else:
        slim = lax.psum_scatter(slim, "y", scatter_dimension=1, tiled=False)
    at = 3 * heads_n // ny
    grad_head = slim[:, :at].reshape(LAYERS, 3, -1)
    grad_ffn = slim[:, at:]

    total = jnp.stack([sums[layer][:3] for layer in range(LAYERS)])
    total = total + swap(total, "x")
    total = total + swap(total, "c")
    if ny == 2:
        half = D // 2
        total = total[..., :half] + swap(total[..., half:], "y")
    else:
        total = lax.psum_scatter(total, "y", scatter_dimension=2, tiled=True)
    grad_model = lax.dynamic_slice_in_dim(total, place.z * dd, dd, 2)
    for k in range(1, ZS):
        grad_model = grad_model + shift_z(
            lax.dynamic_slice_in_dim(total, (place.z + k) % ZS * dd, dd, 2), k
        )
    grad_model = jnp.concatenate([grad_model, grad_model[:, 2:]], 1)

    small = []
    for weight, grad, first, second in (
        (vec_model, grad_model, first_model, second_model),
        (vec_head, grad_head, first_head, second_head),
        (vec_ffn, grad_ffn, first_ffn, second_ffn),
    ):
        small.append(grad)
        small.extend(adamw(weight, grad, first, second, 0.6, 0.0))
    ones, twos = outs["front"], outs["back"]
    return (
        result_rows,
        give(place, [low, swap(low, "c"), low_x, swap(low_x, "c")]),
        *ones[:4],
        *twos[:4],
        *ones[4:],
        *twos[4:],
        *small,
    )


def solution(mesh):
    n_dp, n_mp = mesh.devices.shape
    ny = n_dp // ZS
    split = Mesh(mesh.devices.reshape(ZS, ny, n_mp // 2, 2), ("z", "y", "x", "c"))
    dp, mp = ("z", "y"), ("x", "c")
    both = ("x", "c", "z", "y")
    params = (
        P(None, None, dp, mp),
        P(None, mp, dp),
        P(None, dp, mp),
        P(None, mp, dp),
        P(None, None, dp),
        P(None, None, both),
        P(None, both),
    )
    tokens = (P(dp, None), P(dp, None))
    return jax.shard_map(
        lambda *arrays: per_device(ny, *arrays),
        mesh=split,
        in_specs=(*tokens, P(dp), *params, *params, *params),
        out_specs=(*tokens, *(spec for spec in params for _ in range(4))),
        check_vma=False,
    )
```
